32 devices in a mesh: head: 2 (over x), blk: 16 (over z, y, core).
Axes of the slice: x: 2, y: 2, z: 4, core: 2. Of those that a mesh axis runs over, the one named last changes fastest.
Arguments:
- query_act: bfloat16 [4096, 5120], P(('blk', 'head')), may hold values from -6 to 6
- key_act: bfloat16 [4096, 1024], P(('blk', 'head')), may hold values from -6 to 6
- value_act: bfloat16 [4096, 1024], P(('blk', 'head')), may hold values from -6 to 6
- attn_out: bfloat16 [4096, 5120], P(('blk', 'head')), may hold values from -4 to 4
- grad_out: bfloat16 [4096, 5120], P(('blk', 'head')), may hold values from -6 to 6
- log_sum: float32 [4096, 40], P(('blk', 'head')), may hold values from 5 to 6.5
- kv_lists: int32 [32, 32], P('blk'), may hold values from -1 to 31, as said below
Outputs:
- grad_query: bfloat16 [4096, 5120], P(('blk', 'head'))
- grad_key: bfloat16 [4096, 1024], P(('blk', 'head'))
- grad_value: bfloat16 [4096, 1024], P(('blk', 'head'))
The draws below stay inside these ranges and needn't reach their ends.
Inputs may be any that keep to these rules, and one draw needn't show every extreme that they name: `kv_lists`: the pack is made of prompt trees: the first holds 16 blocks, the last 16, and those between 32 blocks each, in order. A tree is a prompt, then branches. Row r names in rising order the blocks whose keys block r sees (the tree's prompt blocks up to r, and the earlier blocks of r's branch), then -1 to the end. Every entry lies in the same tree as r and is at most r; r itself is always named.
All inputs are finite; a program needn't handle non-finite values.
Results may differ from the reference program's by a relative error of at most 0.0049.
Values may be sent and summed in bfloat16 or wider, within the bound.
No kernel may reach another device: no remote copies, remote signals or barrier semaphores. Data moves between devices by JAX's collectives and lax.ppermute only.
A program may use at most 64 MiB of HBM per device.

```python
import jax
import jax.numpy as jnp
from jax import lax

QH = 40
KVH = 8
HD = 128
BLOCK = 128
TREE_B = 32
SEQ = 4096


def draw_kv_lists(key, part):
    total_blocks = SEQ // BLOCK
    half_tree = TREE_B // 2
    trees = total_blocks // TREE_B + 1
    key_prefix, key_cut = jax.random.split(jax.random.fold_in(key, 17), 2)
    prefix = jax.random.randint(key_prefix, (trees, 1), 1, TREE_B // 4 + 1).astype(jnp.int32)
    cuts = jax.random.randint(key_cut, (trees, TREE_B), 0, 6) == 0
    spots = jnp.arange(TREE_B, dtype=jnp.int32)[None, :]
    branch_starts = (spots == prefix) | (spots > prefix) & cuts
    branch_table = lax.cummax(jnp.where(branch_starts, spots, 0).astype(jnp.int32), axis=1)
    blocks = jnp.arange(total_blocks, dtype=jnp.int32)
    tree_of = (blocks + half_tree) // TREE_B
    tree_start = jnp.maximum(tree_of * TREE_B - half_tree, 0).astype(jnp.int32)
    local = (blocks - tree_start).astype(jnp.int32)
    block_prefix = jnp.take(prefix[:, 0], tree_of)
    block_branch = branch_table[tree_of, local]
    cols = jnp.arange(TREE_B, dtype=jnp.int32)[None, :]
    seen = (cols <= local[:, None]) & ((cols < block_prefix[:, None]) | (cols >= block_branch[:, None]))
    order = jnp.argsort(jnp.where(seen, 0, 1).astype(jnp.int32), axis=1, stable=True).astype(jnp.int32)
    sorted_seen = jnp.take_along_axis(seen, order, axis=1)
    lists = jnp.where(sorted_seen, tree_start[:, None] + order, -1).astype(jnp.int32)
    return lists


def block_scale(stream_key, dims, cuts, least, top_value):
    factor_of = 1.0
    for dim, blocks in cuts:
        steps = jax.random.uniform(jax.random.fold_in(jax.random.fold_in(stream_key, 6), dim), (blocks,), jnp.float32, least / len(cuts), top_value / len(cuts))
        factor_of = factor_of * jnp.repeat(jnp.exp(steps), dims[dim] // blocks).reshape((-1,) + (1,) * (len(dims) - 1 - dim))
    return factor_of


def normal_values(own_key, shape, deviation, limit, pieces=(), kind=jnp.bfloat16):
    entries = deviation * jax.random.normal(own_key, shape, jnp.float32)
    if pieces:
        entries = entries * block_scale(own_key, shape, pieces, -0.22, 0.18)
    return jnp.clip(entries, -limit, limit).astype(kind)


def setup_inputs(seed: int = 0) -> dict:
    seeds = jax.random.split(jax.random.key(seed), 8)
    return {
        "query_act": normal_values(seeds[0], (SEQ, QH * HD), 1.0, 6.0, ((0, 32),)),
        "key_act": normal_values(seeds[1], (SEQ, KVH * HD), 1.0, 6.0, ((0, 32),)),
        "value_act": normal_values(seeds[2], (SEQ, KVH * HD), 1.0, 6.0, ((0, 32),)),
        "attn_out": normal_values(seeds[3], (SEQ, QH * HD), 0.5, 4.0, ((0, 32),)),
        "grad_out": normal_values(seeds[4], (SEQ, QH * HD), 1.0, 6.0, ((0, 32),)),
        "log_sum": jnp.clip(5.0 + 1.5 * jax.random.uniform(seeds[5], (SEQ, QH), jnp.float32) ** block_scale(seeds[5], (SEQ, QH), ((0, 32),), -0.2, 0.2), 5.0, 6.5),
        "kv_lists": draw_kv_lists(jax.random.fold_in(seeds[7], 71), 0),
    }


def head_major(rows, heads):
    return rows.astype(jnp.float32).reshape(SEQ, heads, HD).transpose(1, 0, 2)


def rounded(values):
    return lax.optimization_barrier(values.astype(jnp.bfloat16)).astype(jnp.float32)


def reference(query_act, key_act, value_act, attn_out, grad_out, log_sum, kv_lists):
    group_size = QH // KVH
    scaling = HD ** -0.5
    tile_rows = min(512, SEQ)
    window = min(SEQ, tile_rows + (TREE_B - 1) * BLOCK)
    highest = lax.Precision.HIGHEST
    queries = head_major(query_act, QH).reshape(KVH, group_size, SEQ, HD)
    out_grads = head_major(grad_out, QH).reshape(KVH, group_size, SEQ, HD)
    outputs = head_major(attn_out, QH).reshape(KVH, group_size, SEQ, HD)
    row_delta = jnp.sum(out_grads * outputs, axis=3)
    row_totals = log_sum.astype(jnp.float32).T.reshape(KVH, group_size, SEQ)
    key_heads = head_major(key_act, KVH)
    value_heads = head_major(value_act, KVH)
    tile_starts = jnp.arange(SEQ // tile_rows, dtype=jnp.int32) * tile_rows

    def one_head(operands):
        query_head, grad_head, key_head, value_head, totals, deltas = operands

        def tile_step(carried, tile_start):
            key_sum, value_sum = carried
            query_tile = lax.dynamic_slice_in_dim(query_head, tile_start, tile_rows, 1)
            grad_tile = lax.dynamic_slice_in_dim(grad_head, tile_start, tile_rows, 1)
            total_tile = lax.dynamic_slice_in_dim(totals, tile_start, tile_rows, 1)
            delta_tile = lax.dynamic_slice_in_dim(deltas, tile_start, tile_rows, 1)
            win_start = jnp.clip(tile_start - (TREE_B - 1) * BLOCK, 0, SEQ - window).astype(jnp.int32)
            key_win = lax.dynamic_slice_in_dim(key_head, win_start, window, 0)
            value_win = lax.dynamic_slice_in_dim(value_head, win_start, window, 0)
            row_lists = lax.dynamic_slice_in_dim(kv_lists, (tile_start // BLOCK).astype(jnp.int32), tile_rows // BLOCK, 0)
            key_ids = (win_start // BLOCK).astype(jnp.int32) + jnp.arange(window // BLOCK, dtype=jnp.int32)
            listed = jnp.any(row_lists[:, :, None] == key_ids[None, None, :], axis=1)
            listed = jnp.repeat(jnp.repeat(listed, BLOCK, axis=0), BLOCK, axis=1)
            query_pos = tile_start + jnp.arange(tile_rows, dtype=jnp.int32)
            key_pos = win_start + jnp.arange(window, dtype=jnp.int32)
            visible = listed & (key_pos[None, :] <= query_pos[:, None])
            scores = jnp.einsum("gtd,sd->gts", query_tile, key_win, precision=highest) * scaling
            weights = jnp.where(visible[None], jnp.exp(scores - total_tile[:, :, None]), 0.0)
            grad_probs = jnp.einsum("gtd,sd->gts", grad_tile, value_win, precision=highest)
            grad_scores = rounded(weights * (grad_probs - delta_tile[:, :, None]))
            probs_low = rounded(weights)
            query_part = jnp.einsum("gts,sd->gtd", grad_scores, key_win, precision=highest) * scaling
            key_part = jnp.einsum("gts,gtd->sd", grad_scores, query_tile, precision=highest) * scaling
            value_part = jnp.einsum("gts,gtd->sd", probs_low, grad_tile, precision=highest)
            key_old = lax.dynamic_slice_in_dim(key_sum, win_start, window, 0)
            value_old = lax.dynamic_slice_in_dim(value_sum, win_start, window, 0)
            key_sum = lax.dynamic_update_slice_in_dim(key_sum, key_old + key_part, win_start, 0)
            value_sum = lax.dynamic_update_slice_in_dim(value_sum, value_old + value_part, win_start, 0)
            return (key_sum, value_sum), query_part

        empty_sum = jnp.zeros((SEQ, HD), jnp.float32)
        (key_sum, value_sum), query_parts = lax.scan(tile_step, (empty_sum, empty_sum), tile_starts)
        query_grad = query_parts.transpose(1, 0, 2, 3).reshape(group_size, SEQ, HD)
        return query_grad, key_sum, value_sum

    query_grad, key_grad, value_grad = lax.map(one_head, (queries, out_grads, key_heads, value_heads, row_totals, row_delta))
    grad_query = query_grad.transpose(2, 0, 1, 3).reshape(SEQ, QH * HD).astype(jnp.bfloat16)
    grad_key = key_grad.transpose(1, 0, 2).reshape(SEQ, KVH * HD).astype(jnp.bfloat16)
    grad_value = value_grad.transpose(1, 0, 2).reshape(SEQ, KVH * HD).astype(jnp.bfloat16)
    return (grad_query, grad_key, grad_value)
```

```python
import functools
import math

import jax
import jax.numpy as jnp
from jax import lax
from jax.experimental import pallas as pl
from jax.experimental.pallas import tpu as pltpu
from jax.sharding import PartitionSpec as P

QH = 40
KVH = 8
HD = 128
BLOCK = 128
TREE_B = 32
GROUP = QH // KVH
SCALING = HD ** (-0.5)
F32 = jnp.float32
BF16 = jnp.bfloat16

Q_ROWS = GROUP * BLOCK
K_AT = 2 * Q_ROWS
V_AT = K_AT + BLOCK
X_AT = V_AT + BLOCK
X_ROWS = 64
SEND_ROWS = X_AT + X_ROWS
BACK_ROWS = Q_ROWS + 2 * BLOCK


def dot_nt(a, b):
    return lax.dot_general(a, b, (((1,), (1,)), ((), ())), preferred_element_type=F32)


def dot_nn(a, b):
    return lax.dot_general(a, b, (((1,), (0,)), ((), ())), preferred_element_type=F32)


def three_parts(array):
    high = array.astype(BF16)
    rest = array - high.astype(F32)
    middle = rest.astype(BF16)
    return high, middle, (rest - middle.astype(F32)).astype(BF16)


def pack_kernel(query, key, value, out, grad, totals, row, packed, totals_t):
    group = pl.program_id(0)

    @pl.when(group == 0)
    def _():
        wide = jnp.concatenate([totals[...], jnp.zeros((BLOCK, HD - QH), F32)], axis=1)
        flipped = wide.T
        totals_t[...] = jnp.zeros(totals_t.shape, F32)
        for g in range(KVH):
            totals_t[g, :GROUP, :] = flipped[g * GROUP : (g + 1) * GROUP, :]

    for h in range(GROUP):
        packed[0, h * BLOCK : (h + 1) * BLOCK, :] = query[:, h * HD : (h + 1) * HD]
        packed[0, Q_ROWS + h * BLOCK : Q_ROWS + (h + 1) * BLOCK, :] = grad[:, h * HD : (h + 1) * HD]
    packed[0, K_AT:V_AT, :] = key[...]
    packed[0, V_AT:X_AT, :] = value[...]
    product = grad[...].astype(F32) * out[...].astype(F32)
    high = product.astype(BF16)
    low = (product - high.astype(F32)).astype(BF16)
    picks = (
        lax.broadcasted_iota(jnp.int32, (8, GROUP * HD), 1) // HD
        == lax.broadcasted_iota(jnp.int32, (8, GROUP * HD), 0)
    )
    picks = jnp.where(picks, 1.0, 0.0).astype(BF16)
    delta = dot_nt(picks, high) + dot_nt(picks, low)
    parts = three_parts(jnp.concatenate([totals_t[group], delta], axis=0))
    for i, part in enumerate(parts):
        packed[0, X_AT + 16 * i : X_AT + 16 * (i + 1), :] = part
    packed[0, X_AT + 48 :, :] = jnp.broadcast_to(row[...], (16, HD)).astype(BF16)


def pack(query_act, key_act, value_act, attn_out, grad_out, log_sum, list_row):
    wide = pl.BlockSpec((BLOCK, GROUP * HD), lambda g: (0, g))
    narrow = pl.BlockSpec((BLOCK, HD), lambda g: (0, g))
    return pl.pallas_call(
        pack_kernel,
        grid=(KVH,),
        out_shape=jax.ShapeDtypeStruct((KVH, SEND_ROWS, HD), BF16),
        in_specs=[
            wide,
            narrow,
            narrow,
            wide,
            wide,
            pl.BlockSpec((BLOCK, QH), lambda g: (0, 0)),
            pl.BlockSpec((1, HD), lambda g: (0, 0)),
        ],
        out_specs=pl.BlockSpec((1, SEND_ROWS, HD), lambda g: (g, 0, 0)),
        scratch_shapes=[pltpu.VMEM((KVH, 8, HD), F32)],
        compiler_params=pltpu.CompilerParams(vmem_limit_bytes=32 << 20),
    )(query_act, key_act, value_act, attn_out, grad_out, log_sum, list_row)


def attend_kernel(lists, place, sent, kv_other, query_grad, mine, others, keys, keys_t, values, key_sum, value_sum, query_sum):
    step = pl.program_id(0)
    steps = pl.num_programs(0)
    parity = place[0]
    count = 2 * steps

    @pl.when(step == 0)
    def _():
        def take(p, _):
            for k, v, at in (
                (sent[p, K_AT:V_AT, :], sent[p, V_AT:X_AT, :], 2 * p + parity),
                (kv_other[p, :BLOCK, :], kv_other[p, BLOCK:, :], 2 * p + 1 - parity),
            ):
                keys[at] = k
                values[at] = v
                keys_t[at] = k.astype(F32).T.astype(BF16)
            return 0

        lax.fori_loop(0, steps, take, 0)

        def clear(j, _):
            key_sum[j] = jnp.zeros((BLOCK, HD), F32)
            value_sum[j] = jnp.zeros((BLOCK, HD), F32)
            return 0

        lax.fori_loop(0, count, clear, 0)

    queries = sent[step, :Q_ROWS, :]
    grads = sent[step, Q_ROWS:K_AT, :]
    extras = (
        sent[step, X_AT : X_AT + 16, :].astype(F32)
        + sent[step, X_AT + 16 : X_AT + 32, :].astype(F32)
        + sent[step, X_AT + 32 : X_AT + 48, :].astype(F32)
    )
    totals = jnp.concatenate([extras[h : h + 1, :] for h in range(GROUP)], axis=1) * math.log2(math.e)
    deltas = jnp.concatenate([extras[8 + h : 9 + h, :] for h in range(GROUP)], axis=1)
    query_sum[...] = jnp.zeros((HD, Q_ROWS), F32)

    def tile(j, diagonal):
        k, v = keys[j], values[j]
        scores = dot_nt(k, queries)
        probs = jnp.exp2(scores * (SCALING * math.log2(math.e)) - totals)
        if diagonal:
            at_key = lax.broadcasted_iota(jnp.int32, (BLOCK, Q_ROWS), 0)
            at_query = lax.broadcasted_iota(jnp.int32, (BLOCK, Q_ROWS), 1) % BLOCK
            probs = jnp.where(at_key <= at_query, probs, 0.0)
        grad_probs = dot_nt(v, grads)
        grad_scores = (probs * (grad_probs - deltas)).astype(BF16)
        value_sum[j] += dot_nn(probs.astype(BF16), grads)
        key_sum[j] += dot_nn(grad_scores, queries)
        query_sum[...] += dot_nn(keys_t[j], grad_scores)

    own = 2 * step + parity

    def visit(t, _):
        j = lists[step, t]

        @pl.when((j >= 0) & (j < own))
        def _():
            tile(j, False)

        return 0

    lax.fori_loop(0, own, visit, 0)
    tile(own, True)
    for h in range(GROUP):
        part = query_sum[:, h * BLOCK : (h + 1) * BLOCK].T
        query_grad[0, h * BLOCK : (h + 1) * BLOCK, :] = (part * SCALING).astype(BF16)

    @pl.when(step == steps - 1)
    def _():
        def give(p, _):
            at = 2 * p + parity
            mine[p, :BLOCK, :] = key_sum[at] * SCALING
            mine[p, BLOCK:, :] = value_sum[at]
            at = 2 * p + 1 - parity
            others[p, :BLOCK, :] = key_sum[at] * SCALING
            others[p, BLOCK:, :] = value_sum[at]
            return 0

        lax.fori_loop(0, steps, give, 0)


def attend(lists, place, sent, kv_other):
    steps = sent.shape[0]
    whole = lambda *dims: pl.BlockSpec(dims, lambda p, *_: (0,) * len(dims))
    return pl.pallas_call(
        attend_kernel,
        grid_spec=pltpu.PrefetchScalarGridSpec(
            num_scalar_prefetch=2,
            grid=(steps,),
            in_specs=[whole(steps, SEND_ROWS, HD), whole(steps, 2 * BLOCK, HD)],
            out_specs=[
                pl.BlockSpec((1, Q_ROWS, HD), lambda p, *_: (p, 0, 0)),
                whole(steps, 2 * BLOCK, HD),
                whole(steps, 2 * BLOCK, HD),
            ],
            scratch_shapes=[
                pltpu.VMEM((2 * steps, BLOCK, HD), BF16),
                pltpu.VMEM((2 * steps, BLOCK, HD), BF16),
                pltpu.VMEM((2 * steps, BLOCK, HD), BF16),
                pltpu.VMEM((2 * steps, BLOCK, HD), F32),
                pltpu.VMEM((2 * steps, BLOCK, HD), F32),
                pltpu.VMEM((HD, Q_ROWS), F32),
            ],
        ),
        out_shape=[
            jax.ShapeDtypeStruct((steps, Q_ROWS, HD), BF16),
            jax.ShapeDtypeStruct((steps, 2 * BLOCK, HD), F32),
            jax.ShapeDtypeStruct((steps, 2 * BLOCK, HD), F32),
        ],
        compiler_params=pltpu.CompilerParams(vmem_limit_bytes=48 << 20),
    )(lists, place, sent, kv_other)


def unpack_kernel(back, query_grad, key_grad, value_grad):
    for h in range(GROUP):
        query_grad[:, h * HD : (h + 1) * HD] = back[0, h * BLOCK : (h + 1) * BLOCK, :]
    key_grad[...] = back[0, Q_ROWS : Q_ROWS + BLOCK, :]
    value_grad[...] = back[0, Q_ROWS + BLOCK :, :]


def unpack(back):
    wide = pl.BlockSpec((BLOCK, GROUP * HD), lambda g: (0, g))
    narrow = pl.BlockSpec((BLOCK, HD), lambda g: (0, g))
    return pl.pallas_call(
        unpack_kernel,
        grid=(KVH,),
        out_shape=[
            jax.ShapeDtypeStruct((BLOCK, QH * HD), BF16),
            jax.ShapeDtypeStruct((BLOCK, KVH * HD), BF16),
            jax.ShapeDtypeStruct((BLOCK, KVH * HD), BF16),
        ],
        in_specs=[pl.BlockSpec((1, BACK_ROWS, HD), lambda g: (g, 0, 0))],
        out_specs=[wide, narrow, narrow],
        compiler_params=pltpu.CompilerParams(vmem_limit_bytes=32 << 20),
    )(back)


def by_trees(query_act, key_act, value_act, attn_out, grad_out, log_sum, kv_lists):
    blk_count = lax.axis_size("blk")
    position = lax.axis_index("blk")
    parity = lax.axis_index("head")
    groups = [list(range(at, at + KVH)) for at in range(0, blk_count, KVH)]
    first = (position // KVH) * KVH * lax.axis_size("head")
    row = lax.dynamic_slice_in_dim(kv_lists, parity, 1, 0)
    row = jnp.where(row >= 0, row - first, -1).astype(F32)
    row = jnp.pad(row, ((0, 0), (0, HD - row.shape[1])), constant_values=-1.0)
    packed = pack(query_act, key_act, value_act, attn_out, grad_out, log_sum, row)
    sent = lax.all_to_all(packed, "blk", 0, 0, axis_index_groups=groups, tiled=True)
    kv_other = lax.ppermute(sent[:, K_AT:X_AT, :], "head", [(0, 1), (1, 0)])
    lists = sent[:, X_AT + 48, :TREE_B].astype(jnp.int32)
    query_grad, mine, others = attend(lists, parity.astype(jnp.int32).reshape(1), sent, kv_other)
    arrived = lax.ppermute(others, "head", [(0, 1), (1, 0)])
    back = jnp.concatenate([query_grad, (mine + arrived).astype(BF16)], axis=1)
    back = lax.all_to_all(back, "blk", 0, 0, axis_index_groups=groups, tiled=True)
    return tuple(unpack(back))


def passed_along(array, axis, by):
    size = lax.axis_size(axis)
    pairs = [(i, i + by) for i in range(size) if 0 <= i + by < size]
    return lax.ppermute(array, axis, pairs)


def shifted(array, axis, by):
    size = lax.axis_size(axis)
    return lax.ppermute(array, axis, [(i, (i + by) % size) for i in range(size)])


def head_delta(grad_rows, out_rows, heads):
    count = grad_rows.shape[0]
    return jnp.einsum(
        "thd,thd->th",
        grad_rows.reshape(count, heads, HD),
        out_rows.reshape(count, heads, HD),
        preferred_element_type=jnp.float32,
    )


def by_ring(query_act, key_act, value_act, attn_out, grad_out, log_sum, kv_lists):
    head_count = lax.axis_size("head")
    blk_count = lax.axis_size("blk")
    sent_delta = head_delta(grad_out, attn_out, QH)
    query_rows, key_rows, value_rows, grad_rows, total_rows, delta_rows = (
        lax.all_to_all(
            query_act.astype(jnp.float32), "head", split_axis=1, concat_axis=0, tiled=True
        ).astype(query_act.dtype),
        lax.all_to_all(
            key_act.astype(jnp.float32), "head", split_axis=1, concat_axis=0, tiled=True
        ).astype(key_act.dtype),
        lax.all_to_all(
            value_act.astype(jnp.float32), "head", split_axis=1, concat_axis=0, tiled=True
        ).astype(value_act.dtype),
        lax.all_to_all(
            grad_out.astype(jnp.float32), "head", split_axis=1, concat_axis=0, tiled=True
        ).astype(grad_out.dtype),
        lax.all_to_all(log_sum, "head", split_axis=1, concat_axis=0, tiled=True),
        lax.all_to_all(sent_delta, "head", split_axis=1, concat_axis=0, tiled=True),
    )
    tokens = query_rows.shape[0]
    local_heads = KVH // head_count
    group_size = QH // KVH
    blocks_dev = tokens // BLOCK
    scaling = HD ** (-0.5)
    queries = query_rows.reshape(tokens, local_heads, group_size, HD)
    out_grads = grad_rows.reshape(tokens, local_heads, group_size, HD)
    row_totals = total_rows.reshape(tokens, local_heads, group_size).transpose(1, 2, 0)[
        :, :, :, None
    ]
    row_deltas = delta_rows.reshape(tokens, local_heads, group_size).transpose(1, 2, 0)[
        :, :, :, None
    ]
    position = lax.axis_index("blk")
    query_pos = position * tokens + jnp.arange(tokens, dtype=jnp.int32)

    def block_mask(rotation):
        source = (position - rotation) % blk_count
        key_ids = source * blocks_dev + jnp.arange(blocks_dev, dtype=jnp.int32)
        listed = jnp.any(kv_lists[:, :, None] == key_ids[None, None, :], axis=1)
        key_pos = source * tokens + jnp.arange(tokens, dtype=jnp.int32)
        return (listed, key_pos)

    def attend(kv_pair, key_sums, query_grad, listed, key_pos):
        visible = jnp.repeat(jnp.repeat(listed, BLOCK, axis=0), BLOCK, axis=1) & (
            key_pos[None, :] <= query_pos[:, None]
        )
        key_block = kv_pair[0].reshape(tokens, local_heads, HD)
        value_block = kv_pair[1].reshape(tokens, local_heads, HD)
        scores = (
            jnp.einsum("tkgd,skd->kgts", queries, key_block, preferred_element_type=jnp.float32)
            * scaling
        )
        weights = jnp.where(visible, jnp.exp(scores - row_totals), 0.0)
        grad_probs = jnp.einsum(
            "tkgd,skd->kgts", out_grads, value_block, preferred_element_type=jnp.float32
        )
        grad_scores = (weights * (grad_probs - row_deltas)).astype(jnp.bfloat16)
        probs_low = weights.astype(jnp.bfloat16)
        value_part = jnp.einsum(
            "kgts,tkgd->skd", probs_low, out_grads, preferred_element_type=jnp.float32
        )
        key_part = (
            jnp.einsum("kgts,tkgd->skd", grad_scores, queries, preferred_element_type=jnp.float32)
            * scaling
        )
        query_part = (
            jnp.einsum("kgts,skd->tkgd", grad_scores, key_block, preferred_element_type=jnp.float32)
            * scaling
        )
        added = jnp.stack(
            [
                key_part.reshape(tokens, local_heads * HD),
                value_part.reshape(tokens, local_heads * HD),
            ]
        )
        return (key_sums + added, query_grad + query_part)

    def visit(rotation, kv_pair, key_sums, query_grad):
        listed, key_pos = block_mask(rotation)
        return attend(kv_pair, key_sums, query_grad, listed, key_pos)

    kv_pair = jnp.stack([key_rows, value_rows])
    empty_sums = jnp.zeros((2, tokens, local_heads * HD), jnp.float32)
    empty_grad = jnp.zeros((tokens, local_heads, group_size, HD), jnp.float32)

    def advance(rotation, carried):
        kv_here, key_sums, query_grad = carried
        arrived = passed_along(kv_here, "blk", 1)
        key_sums, query_grad = visit(rotation, kv_here, key_sums, query_grad)
        key_sums = shifted(key_sums, "blk", 1)
        return (arrived, key_sums, query_grad)

    kv_here, key_sums, query_grad = lax.fori_loop(
        0, blk_count - 1, advance, (kv_pair, empty_sums, empty_grad)
    )
    key_sums, query_grad = visit(blk_count - 1, kv_here, key_sums, query_grad)
    key_sums = shifted(key_sums.astype(jnp.bfloat16), "blk", 1 - blk_count).astype(key_sums.dtype)
    query_low = query_grad.reshape(tokens, local_heads * group_size * HD).astype(jnp.bfloat16)
    key_low = key_sums[0].astype(jnp.bfloat16)
    value_low = key_sums[1].astype(jnp.bfloat16)
    grad_query, grad_key, grad_value = (
        lax.all_to_all(query_low, "head", split_axis=0, concat_axis=1, tiled=True),
        lax.all_to_all(key_low, "head", split_axis=0, concat_axis=1, tiled=True),
        lax.all_to_all(value_low, "head", split_axis=0, concat_axis=1, tiled=True),
    )
    return (grad_query, grad_key, grad_value)


def local(query_act, *others):
    head_count = lax.axis_size("head")
    blk_count = lax.axis_size("blk")
    if query_act.shape[0] == BLOCK and head_count == 2 and blk_count == 2 * KVH and blk_count * head_count == TREE_B:
        return by_trees(query_act, *others)
    return by_ring(query_act, *others)


def solution(mesh):
    rows = P(("blk", "head"), None)
    return jax.shard_map(
        local,
        mesh=mesh,
        in_specs=(rows,) * 6 + (P("blk", None),),
        out_specs=(rows,) * 3,
        check_vma=False,
    )
```

```python
import functools
import math

import jax
import jax.numpy as jnp
from jax import lax
from jax.experimental import pallas as pl
from jax.experimental.pallas import tpu as pltpu
from jax.sharding import PartitionSpec as P

QH = 40
KVH = 8
HD = 128
BLOCK = 128
TREE_B = 32
GROUP = QH // KVH
SCALING = HD ** (-0.5)
F32 = jnp.float32
BF16 = jnp.bfloat16

Q_ROWS = GROUP * BLOCK
LIST_AT = 2 * BLOCK
KV_ROWS = LIST_AT + 16
X_AT = 2 * Q_ROWS
QG_ROWS = X_AT + 48
COUNT_COL = TREE_B
OWN_COL = TREE_B + 1
VMEM_LIMIT = 20 << 20


def dot_nt(a, b):
    return lax.dot_general(a, b, (((1,), (1,)), ((), ())), preferred_element_type=F32)


def dot_nn(a, b):
    return lax.dot_general(a, b, (((1,), (0,)), ((), ())), preferred_element_type=F32)


def three_parts(array):
    high = array.astype(BF16)
    rest = array - high.astype(F32)
    middle = rest.astype(BF16)
    return high, middle, (rest - middle.astype(F32)).astype(BF16)


def in_vmem(count):
    return [pl.BlockSpec(memory_space=pltpu.VMEM)] * count


def call(kernel, name, in_specs, outs, scratch, micros, args, after=(), limit=VMEM_LIMIT):
    given = len(args)

    def body(*refs):
        kernel(*refs[:given], *refs[given + len(after) :])

    return pl.pallas_call(
        body,
        name=name,
        in_specs=[*in_specs, *[pl.BlockSpec(memory_space=pl.ANY)] * len(after)],
        out_specs=in_vmem(len(outs)),
        out_shape=[jax.ShapeDtypeStruct(*out) for out in outs],
        scratch_shapes=scratch,
        cost_estimate=pl.CostEstimate(flops=int(micros * 1e9), bytes_accessed=int(micros * 3e6), transcendentals=0),
        compiler_params=pltpu.CompilerParams(vmem_limit_bytes=limit),
    )(*args, *after)


def kv_pack_kernel(key_in, value_in, lists_in, kept, given, rows, key, value, lists, arrived):
    copies = [
        pltpu.make_async_copy(source, target, arrived.at[i])
        for i, (source, target) in enumerate(((lists_in, lists), (key_in, key), (value_in, value)))
    ]
    for copy in copies:
        copy.start()
    position, parity = lax.axis_index("blk"), lax.axis_index("head")
    me = lax.rem(position, KVH)
    first = (position - me) * 2
    rows[...] = jnp.full(rows.shape, -1.0, F32)
    for copy in copies:
        copy.wait()
    rows[:2, :TREE_B] = lists[...].astype(F32)
    row = jnp.where(parity == 0, rows[0:1, :], rows[1:2, :])
    seen = row >= 0
    count = jnp.sum(jnp.where(seen, 1.0, 0.0)) - 1.0
    lane = lax.broadcasted_iota(jnp.int32, row.shape, 1)
    row = jnp.where(seen, row - first.astype(F32), -1.0)
    row = jnp.where(lane == COUNT_COL, count, row)
    row = jnp.where(lane == OWN_COL, (2 * me + parity).astype(F32), row)
    tile = jnp.broadcast_to(row, (KV_ROWS - LIST_AT, HD)).astype(BF16)
    for i, chip in enumerate(CHIPS):
        for k, target in ((chip, kept), (chip + 1, given)):
            columns = pl.ds(pl.multiple_of((me ^ k) * HD, HD), HD)
            target[i, :BLOCK, :] = key[:, columns]
            target[i, BLOCK:LIST_AT, :] = value[:, columns]
            target[i, LIST_AT:, :] = tile


def kv_pack(key_act, value_act, kv_lists):
    outs = [((len(CHIPS), KV_ROWS, HD), BF16)] * 2
    args = (key_act, value_act, kv_lists)
    scratch = [pltpu.VMEM((8, HD), F32), *(pltpu.VMEM(arg.shape, arg.dtype) for arg in args), pltpu.SemaphoreType.DMA((3,))]
    specs = [pl.BlockSpec(memory_space=pl.ANY)] * 3
    return call(kv_pack_kernel, "kv_pack", specs, outs, scratch, 1, args, limit=60 << 20)


def pair_up_kernel(mine, theirs, *pairs):
    for i, pair in enumerate(pairs):
        pair[0] = mine[i]
        pair[1] = theirs[i]


def pair_up(mine, theirs, after=()):
    outs = [((2, *mine.shape[1:]), mine.dtype)] * mine.shape[0]
    return call(pair_up_kernel, "pair_up", in_vmem(2), outs, [], 0.5, (mine, theirs), after)


def pass_on_kernel(source, target):
    target[...] = source[...]


def pass_on(array, after):
    return call(pass_on_kernel, "pass_on", in_vmem(1), [(array.shape, array.dtype)], [], 0.2, (array,), after)[0]


def kv_sum_kernel(mine, theirs, *sums):
    for i, ref in enumerate(sums):
        ref[...] = (mine[i] + theirs[i].astype(F32)).astype(BF16)


def kv_sum(mine, theirs):
    outs = [(mine.shape[1:], BF16)] * mine.shape[0]
    return call(kv_sum_kernel, "kv_sum", in_vmem(2), outs, [], 0.5, (mine, theirs))


def qg_pack_kernel(slots, query, grad, out, totals, *rest):
    packed, totals_by_group = rest[:-1], rest[-1]
    me = lax.rem(lax.axis_index("blk"), KVH)
    totals_by_group[...] = jnp.zeros(totals_by_group.shape, F32)
    for g in range(KVH):
        totals_by_group[g, :GROUP, :] = totals[g * GROUP : (g + 1) * GROUP, :]
    head_of = lax.broadcasted_iota(jnp.int32, (8, Q_ROWS), 1) // HD
    picks = jnp.where(head_of == lax.broadcasted_iota(jnp.int32, (8, Q_ROWS), 0), 1.0, 0.0).astype(BF16)
    for message, ks in zip(packed, slots):
        for n, k in enumerate(ks):
            columns = pl.ds(pl.multiple_of((me ^ k) * Q_ROWS, Q_ROWS), Q_ROWS)
            queries, grads = query[:, columns], grad[:, columns]
            for h in range(GROUP):
                message[n, h * BLOCK : (h + 1) * BLOCK, :] = queries[:, h * HD : (h + 1) * HD]
                message[n, Q_ROWS + h * BLOCK : Q_ROWS + (h + 1) * BLOCK, :] = grads[:, h * HD : (h + 1) * HD]
            product = grads.astype(F32) * out[:, columns].astype(F32)
            high = product.astype(BF16)
            low = (product - high.astype(F32)).astype(BF16)
            delta = dot_nt(picks, high) + dot_nt(picks, low)
            extras = jnp.concatenate([totals_by_group[me ^ k], delta], axis=0)
            for i, part in enumerate(three_parts(extras)):
                message[n, X_AT + 16 * i : X_AT + 16 * (i + 1), :] = part


def qg_pack(slots, query_act, grad_out, attn_out, totals, after):
    outs = [((len(ks), QG_ROWS, HD), BF16) for ks in slots]
    scratch = [pltpu.VMEM((KVH, 8, HD), F32)]
    args = (query_act, grad_out, attn_out, totals)
    return call(functools.partial(qg_pack_kernel, slots), "qg_pack", in_vmem(4), outs, scratch, 1, args, after)


def attend_kernel(ks, kind, *refs):
    refs = list(refs)
    opens, closes = kind == "first", kind == "last"
    lists = refs.pop(0)
    messages = []
    while len(messages) < len(ks):
        ref = refs.pop(0)
        messages += [ref.at[n] for n in range(ref.shape[0])]
    if opens:
        kv_own, kv_other = [refs.pop(0) for _ in CHIPS], [refs.pop(0) for _ in CHIPS]
    else:
        keys, keys_t, values, sums_in = (refs.pop(0) for _ in range(4))
    if closes:
        earlier = refs.pop(0)
        backs = [refs.pop(0) for _ in ks]
        for n, back in enumerate(backs):
            back[0] = earlier[n]
        query_grads = [back.at[1] for back in backs]
        mine, others = [refs.pop(0) for _ in range(2)], [refs.pop(0) for _ in range(2)]
    else:
        back = refs.pop(0)
        query_grads = [back.at[n] for n in range(len(ks))]
    if opens:
        keys, keys_t, values = (refs.pop(0) for _ in range(3))
    sums = refs.pop(0)
    query_sum, probs_held, scores_held = refs
    me, parity = lists[0, OWN_COL] // 2, lists[0, OWN_COL] % 2
    spare = 2 * KVH

    if opens:
        for own, other, chip in zip(kv_own, kv_other, CHIPS):
            for n in range(2):
                at = 2 * (me ^ (chip + n))
                for ref, j in ((own, at + parity), (other, at + 1 - parity)):
                    keys[j] = ref[n, :BLOCK, :]
                    values[j] = ref[n, BLOCK:LIST_AT, :]
                    keys_t[j] = ref[n, :BLOCK, :].T
        zero = jnp.zeros((BLOCK, HD), BF16)
        keys[spare], keys_t[spare], values[spare] = zero, zero, zero
        sums[...] = jnp.zeros(sums.shape, F32)
    else:
        sums[...] = sums_in[...]

    def both(ref, pair, axis):
        return jnp.concatenate([ref[j] for j in pair], axis=axis)

    def produce(n, pair, extras, diagonal):
        totals, deltas = extras
        scores = dot_nt(both(keys, pair, 0), messages[n][:Q_ROWS, :])
        probs = jnp.exp2(scores * (SCALING * math.log2(math.e)) - totals)
        if diagonal:
            at_key = lax.broadcasted_iota(jnp.int32, probs.shape, 0) - BLOCK
            at_query = lax.broadcasted_iota(jnp.int32, probs.shape, 1) % BLOCK
            probs = jnp.where(at_key <= at_query, probs, 0.0)
        grad_probs = dot_nt(both(values, pair, 0), messages[n][Q_ROWS:X_AT, :])
        probs_held[...] = probs.astype(BF16)
        scores_held[...] = (probs * (grad_probs - deltas)).astype(BF16)

    def consume(n, pair):
        probs_low, grad_scores = probs_held[...], scores_held[...]
        value_part = dot_nn(probs_low, messages[n][Q_ROWS:X_AT, :])
        key_part = dot_nn(grad_scores, messages[n][:Q_ROWS, :])
        query_sum[...] += dot_nn(both(keys_t, pair, 1), grad_scores)
        for i, j in enumerate(pair):
            sums[j, :BLOCK, :] += key_part[i * BLOCK : (i + 1) * BLOCK, :]
            sums[j, BLOCK:, :] += value_part[i * BLOCK : (i + 1) * BLOCK, :]

    def finish(n):
        for h in range(GROUP):
            part = query_sum[:, h * BLOCK : (h + 1) * BLOCK].T
            query_grads[n][h * BLOCK : (h + 1) * BLOCK, :] = (part * SCALING).astype(BF16)

    pair = None
    for n, k in enumerate(ks):
        parts = [messages[n][X_AT + 16 * i : X_AT + 16 * (i + 1), :].astype(F32) for i in range(3)]
        rows = parts[0] + parts[1] + parts[2]
        totals = jnp.concatenate([rows[h : h + 1, :] for h in range(GROUP)], axis=1) * math.log2(math.e)
        deltas = jnp.concatenate([rows[8 + h : 9 + h, :] for h in range(GROUP)], axis=1)
        extras = (totals, deltas)
        count = lists[k, COUNT_COL]
        pairs = count // 2
        left = jnp.where(count % 2 == 1, lists[k, jnp.maximum(count - 1, 0)], spare)
        if pair is not None:
            consume(n - 1, pair)
        produce(n, (left, lists[k, OWN_COL]), extras, True)
        if pair is not None:
            finish(n - 1)
        query_sum[...] = jnp.zeros(query_sum.shape, F32)

        def visit(t, held):
            consume(n, held)
            following = (lists[k, 2 * t], lists[k, 2 * t + 1])
            produce(n, following, extras, False)
            return following

        pair = lax.fori_loop(0, pairs, visit, (left, lists[k, OWN_COL]))
    consume(len(ks) - 1, pair)
    finish(len(ks) - 1)

    if closes:
        for half, own, other in zip(BACK_HALVES, mine, others):
            for i, k in enumerate(half):
                at = 2 * (me ^ k)
                own[i, :BLOCK, :] = sums[at + parity, :BLOCK, :] * SCALING
                own[i, BLOCK:, :] = sums[at + parity, BLOCK:, :]
                other[i, :BLOCK, :] = (sums[at + 1 - parity, :BLOCK, :] * SCALING).astype(BF16)
                other[i, BLOCK:, :] = sums[at + 1 - parity, BLOCK:, :].astype(BF16)


def attend(name, kind, ks, lists, messages, state, micros):
    blocks = 2 * KVH + 1
    sums = ((blocks, 2 * BLOCK, HD), F32)
    scratch = []
    if kind == "last":
        outs = [((2, Q_ROWS, HD), BF16)] * len(ks)
        outs += [((KVH // 2, 2 * BLOCK, HD), kind) for kind in (F32, F32, BF16, BF16)]
        scratch = [pltpu.VMEM(*sums)]
    else:
        outs = [((len(ks), Q_ROWS, HD), BF16)]
        if kind == "first":
            outs += [((blocks, BLOCK, HD), BF16)] * 3
        outs += [sums]
    scratch += [pltpu.VMEM((HD, Q_ROWS), F32), pltpu.VMEM((2 * BLOCK, Q_ROWS), BF16), pltpu.VMEM((2 * BLOCK, Q_ROWS), BF16)]
    specs = [pl.BlockSpec(memory_space=pltpu.SMEM)] + in_vmem(len(messages) + len(state))
    kernel = functools.partial(attend_kernel, ks, kind)
    return call(kernel, name, specs, outs, scratch, micros, (lists, *messages, *state))


def query_relay_kernel(own, *refs):
    given = refs[-1]
    given[0] = own[1]
    for i, back in enumerate(refs[:-1]):
        given[i + 1] = back[1]


def query_unpack_kernel(*refs):
    backs, theirs, query_grad = refs[: len(CHIPS)], refs[len(CHIPS)], refs[len(CHIPS) + 1]
    me = lax.rem(lax.axis_index("blk"), KVH)
    for i, chip in enumerate(CHIPS):
        for k, ref, n in ((chip, backs[i], 0), (chip + 1, theirs, i)):
            for h in range(GROUP):
                columns = pl.ds(pl.multiple_of(((me ^ k) * GROUP + h) * HD, HD), HD)
                query_grad[:, columns] = ref[n, h * BLOCK : (h + 1) * BLOCK, :]


def kv_unpack_kernel(*refs):
    key_grad, value_grad = refs[KVH:]
    me = lax.rem(lax.axis_index("blk"), KVH)
    for k in range(KVH):
        columns = pl.ds(pl.multiple_of((me ^ k) * HD, HD), HD)
        key_grad[:, columns] = refs[k][:BLOCK, :]
        value_grad[:, columns] = refs[k][BLOCK:, :]


CHIPS = (0, 2, 4, 6)
VISITS = (("first", (0, 1)), ("more", (6, 7)), ("more", (2, 4)), ("last", (3, 5)))
EXPECTED = (0.5, 0.5, 0.5, 6)
BACK_HALVES = ((6, 7, 2, 3), (4, 5, 0, 1))


def by_trees(query_act, key_act, value_act, attn_out, grad_out, log_sum, kv_lists):
    size = lax.axis_size("blk")

    def exchanged(array, k):
        return lax.ppermute(array, "blk", [(i, i ^ k) for i in range(size)])

    def swapped(array):
        return lax.ppermute(array, "head", [(0, 1), (1, 0)])

    kept, given = kv_pack(key_act, value_act, kv_lists)
    beside = exchanged(given, 1)
    paired = pair_up(kept, beside)
    kv_own = [paired[0], *(exchanged(part, chip) for part, chip in zip(paired[1:], CHIPS[1:]))]
    kv_other = [swapped(part) for part in kv_own]
    lists = jnp.concatenate([part[:, LIST_AT, : OWN_COL + 1] for part in kv_own]).astype(jnp.int32)

    qg = (query_act, grad_out, attn_out, log_sum.T)
    own, far, given = qg_pack(((0,), (6,), (1, 7)), *qg, (beside,))
    near = exchanged(given, 1)
    far = pair_up(far, near[1:], (*kv_own[1:], kv_other[0]))[0]
    here = {0: (own, near[:1]), 1: (exchanged(far, 6),)}
    sent = dict(zip((2, 4, 3, 5), qg_pack(((2,), (4,), (3,), (5,)), *qg, (far,))))
    here[2] = tuple(exchanged(sent[k], k) for k in (2, 4))
    here[3] = tuple(exchanged(sent[k], k) for k in (3, 5))

    state, grads = (*kv_own, *kv_other), []
    for i, (kind, ks) in enumerate(VISITS):
        if kind == "last":
            state = (*state, grads[-1])
        results = attend(f"attend_{i}", kind, ks, lists, here[i], state, EXPECTED[i])
        grads.append(results[0])
        state = tuple(results[1:]) if kind == "first" else (*state[:3], results[-1])
    far_back = exchanged(grads[1], 6)
    backs = [exchanged(results[0], 2), exchanged(results[1], 4), far_back]
    mine, others = results[2:4], results[4:6]
    theirs = [swapped(pass_on(others[0], (far_back,))), swapped(others[1])]
    kv_back = {}
    for half, own, other in zip(BACK_HALVES, mine, theirs):
        for k, part in zip(half, kv_sum(own, other)):
            kv_back[k] = exchanged(part, k) if k else part
    outs = [((4, Q_ROWS, HD), BF16)]
    given = call(query_relay_kernel, "query_relay", in_vmem(4), outs, [], 0.5, (grads[0], *backs), theirs)[0]
    args = (grads[0], *backs, exchanged(given, 1))
    grad_query = call(query_unpack_kernel, "query_unpack", in_vmem(5), [((BLOCK, QH * HD), BF16)], [], 1, args)
    args = tuple(kv_back[k] for k in range(KVH))
    grad_kv = call(kv_unpack_kernel, "kv_unpack", in_vmem(KVH), [((BLOCK, KVH * HD), BF16)] * 2, [], 1, args, grad_query)
    return (*grad_query, *grad_kv)


def passed_along(array, axis, by):
    size = lax.axis_size(axis)
    pairs = [(i, i + by) for i in range(size) if 0 <= i + by < size]
    return lax.ppermute(array, axis, pairs)


def shifted(array, axis, by):
    size = lax.axis_size(axis)
    return lax.ppermute(array, axis, [(i, (i + by) % size) for i in range(size)])


def head_delta(grad_rows, out_rows, heads):
    count = grad_rows.shape[0]
    return jnp.einsum(
        "thd,thd->th",
        grad_rows.reshape(count, heads, HD),
        out_rows.reshape(count, heads, HD),
        preferred_element_type=jnp.float32,
    )


def by_ring(query_act, key_act, value_act, attn_out, grad_out, log_sum, kv_lists):
    head_count = lax.axis_size("head")
    blk_count = lax.axis_size("blk")
    sent_delta = head_delta(grad_out, attn_out, QH)
    query_rows, key_rows, value_rows, grad_rows, total_rows, delta_rows = (
        lax.all_to_all(
            query_act.astype(jnp.float32), "head", split_axis=1, concat_axis=0, tiled=True
        ).astype(query_act.dtype),
        lax.all_to_all(
            key_act.astype(jnp.float32), "head", split_axis=1, concat_axis=0, tiled=True
        ).astype(key_act.dtype),
        lax.all_to_all(
            value_act.astype(jnp.float32), "head", split_axis=1, concat_axis=0, tiled=True
        ).astype(value_act.dtype),
        lax.all_to_all(
            grad_out.astype(jnp.float32), "head", split_axis=1, concat_axis=0, tiled=True
        ).astype(grad_out.dtype),
        lax.all_to_all(log_sum, "head", split_axis=1, concat_axis=0, tiled=True),
        lax.all_to_all(sent_delta, "head", split_axis=1, concat_axis=0, tiled=True),
    )
    tokens = query_rows.shape[0]
    local_heads = KVH // head_count
    group_size = QH // KVH
    blocks_dev = tokens // BLOCK
    scaling = HD ** (-0.5)
    queries = query_rows.reshape(tokens, local_heads, group_size, HD)
    out_grads = grad_rows.reshape(tokens, local_heads, group_size, HD)
    row_totals = total_rows.reshape(tokens, local_heads, group_size).transpose(1, 2, 0)[
        :, :, :, None
    ]
    row_deltas = delta_rows.reshape(tokens, local_heads, group_size).transpose(1, 2, 0)[
        :, :, :, None
    ]
    position = lax.axis_index("blk")
    query_pos = position * tokens + jnp.arange(tokens, dtype=jnp.int32)

    def block_mask(rotation):
        source = (position - rotation) % blk_count
        key_ids = source * blocks_dev + jnp.arange(blocks_dev, dtype=jnp.int32)
        listed = jnp.any(kv_lists[:, :, None] == key_ids[None, None, :], axis=1)
        key_pos = source * tokens + jnp.arange(tokens, dtype=jnp.int32)
        return (listed, key_pos)

    def attend(kv_pair, key_sums, query_grad, listed, key_pos):
        visible = jnp.repeat(jnp.repeat(listed, BLOCK, axis=0), BLOCK, axis=1) & (
            key_pos[None, :] <= query_pos[:, None]
        )
        key_block = kv_pair[0].reshape(tokens, local_heads, HD)
        value_block = kv_pair[1].reshape(tokens, local_heads, HD)
        scores = (
            jnp.einsum("tkgd,skd->kgts", queries, key_block, preferred_element_type=jnp.float32)
            * scaling
        )
        weights = jnp.where(visible, jnp.exp(scores - row_totals), 0.0)
        grad_probs = jnp.einsum(
            "tkgd,skd->kgts", out_grads, value_block, preferred_element_type=jnp.float32
        )
        grad_scores = (weights * (grad_probs - row_deltas)).astype(jnp.bfloat16)
        probs_low = weights.astype(jnp.bfloat16)
        value_part = jnp.einsum(
            "kgts,tkgd->skd", probs_low, out_grads, preferred_element_type=jnp.float32
        )
        key_part = (
            jnp.einsum("kgts,tkgd->skd", grad_scores, queries, preferred_element_type=jnp.float32)
            * scaling
        )
        query_part = (
            jnp.einsum("kgts,skd->tkgd", grad_scores, key_block, preferred_element_type=jnp.float32)
            * scaling
        )
        added = jnp.stack(
            [
                key_part.reshape(tokens, local_heads * HD),
                value_part.reshape(tokens, local_heads * HD),
            ]
        )
        return (key_sums + added, query_grad + query_part)

    def visit(rotation, kv_pair, key_sums, query_grad):
        listed, key_pos = block_mask(rotation)
        return attend(kv_pair, key_sums, query_grad, listed, key_pos)

    kv_pair = jnp.stack([key_rows, value_rows])
    empty_sums = jnp.zeros((2, tokens, local_heads * HD), jnp.float32)
    empty_grad = jnp.zeros((tokens, local_heads, group_size, HD), jnp.float32)

    def advance(rotation, carried):
        kv_here, key_sums, query_grad = carried
        arrived = passed_along(kv_here, "blk", 1)
        key_sums, query_grad = visit(rotation, kv_here, key_sums, query_grad)
        key_sums = shifted(key_sums, "blk", 1)
        return (arrived, key_sums, query_grad)

    kv_here, key_sums, query_grad = lax.fori_loop(
        0, blk_count - 1, advance, (kv_pair, empty_sums, empty_grad)
    )
    key_sums, query_grad = visit(blk_count - 1, kv_here, key_sums, query_grad)
    key_sums = shifted(key_sums.astype(jnp.bfloat16), "blk", 1 - blk_count).astype(key_sums.dtype)
    query_low = query_grad.reshape(tokens, local_heads * group_size * HD).astype(jnp.bfloat16)
    key_low = key_sums[0].astype(jnp.bfloat16)
    value_low = key_sums[1].astype(jnp.bfloat16)
    grad_query, grad_key, grad_value = (
        lax.all_to_all(query_low, "head", split_axis=0, concat_axis=1, tiled=True),
        lax.all_to_all(key_low, "head", split_axis=0, concat_axis=1, tiled=True),
        lax.all_to_all(value_low, "head", split_axis=0, concat_axis=1, tiled=True),
    )
    return (grad_query, grad_key, grad_value)


def local(query_act, *others):
    head_count = lax.axis_size("head")
    blk_count = lax.axis_size("blk")
    if query_act.shape[0] == BLOCK and head_count == 2 and blk_count == 2 * KVH and blk_count * head_count == TREE_B:
        return by_trees(query_act, *others)
    return by_ring(query_act, *others)


def solution(mesh):
    rows = P(("blk", "head"), None)
    return jax.shard_map(
        local,
        mesh=mesh,
        in_specs=(rows,) * 6 + (P("blk", None),),
        out_specs=(rows,) * 3,
        check_vma=False,
    )
```

```python
import functools
import math

import jax
import jax.numpy as jnp
from jax import lax
from jax.experimental import pallas as pl
from jax.experimental.pallas import tpu as pltpu
from jax.sharding import PartitionSpec as P

QH = 40
KVH = 8
HD = 128
BLOCK = 128
TREE_B = 32
GROUP = QH // KVH
SCALING = HD ** (-0.5)
F32 = jnp.float32
BF16 = jnp.bfloat16

Q_ROWS = GROUP * BLOCK
LIST_AT = 2 * BLOCK
KV_ROWS = LIST_AT + 16
X_AT = 2 * Q_ROWS
QG_ROWS = X_AT + 48
COUNT_COL = TREE_B
OWN_COL = TREE_B + 1
VMEM_LIMIT = 14 << 20


def dot_nt(a, b):
    return lax.dot_general(a, b, (((1,), (1,)), ((), ())), preferred_element_type=F32)


def dot_nn(a, b):
    return lax.dot_general(a, b, (((1,), (0,)), ((), ())), preferred_element_type=F32)


def three_parts(array):
    high = array.astype(BF16)
    rest = array - high.astype(F32)
    middle = rest.astype(BF16)
    return high, middle, (rest - middle.astype(F32)).astype(BF16)


def in_vmem(count):
    return [pl.BlockSpec(memory_space=pltpu.VMEM)] * count


def call(kernel, name, in_specs, outs, scratch, micros, args, after=(), limit=VMEM_LIMIT):
    given = len(args)

    def body(*refs):
        kernel(*refs[:given], *refs[given + len(after) :])

    return pl.pallas_call(
        body,
        name=name,
        in_specs=[*in_specs, *[pl.BlockSpec(memory_space=pl.ANY)] * len(after)],
        out_specs=in_vmem(len(outs)),
        out_shape=[jax.ShapeDtypeStruct(*out) for out in outs],
        scratch_shapes=scratch,
        cost_estimate=pl.CostEstimate(flops=int(micros * 1e9), bytes_accessed=int(micros * 3e6), transcendentals=0),
        compiler_params=pltpu.CompilerParams(vmem_limit_bytes=limit),
    )(*args, *after)


def list_row(lists, rows):
    position, parity = lax.axis_index("blk"), lax.axis_index("head")
    me = lax.rem(position, KVH)
    first = (position - me) * 2
    rows[...] = jnp.full(rows.shape, -1.0, F32)
    rows[:2, :TREE_B] = lists[...].astype(F32)
    row = jnp.where(parity == 0, rows[0:1, :], rows[1:2, :])
    seen = row >= 0
    count = jnp.sum(jnp.where(seen, 1.0, 0.0)) - 1.0
    lane = lax.broadcasted_iota(jnp.int32, row.shape, 1)
    row = jnp.where(seen, row - first.astype(F32), -1.0)
    row = jnp.where(lane == COUNT_COL, count, row)
    row = jnp.where(lane == OWN_COL, (2 * me + parity).astype(F32), row)
    return me, jnp.broadcast_to(row, (KV_ROWS - LIST_AT, HD)).astype(BF16)


def kv_pack_kernel(key_in, value_in, lists_in, given, rows, key, value, lists, arrived):
    copies = [
        pltpu.make_async_copy(source, target, arrived.at[i])
        for i, (source, target) in enumerate(((lists_in, lists), (key_in, key), (value_in, value)))
    ]
    for copy in copies:
        copy.start()
    for copy in copies:
        copy.wait()
    me, tile = list_row(lists, rows)
    for i, chip in enumerate(CHIPS):
        columns = pl.ds(pl.multiple_of((me ^ (chip + 1)) * HD, HD), HD)
        given[i, :BLOCK, :] = key[:, columns]
        given[i, BLOCK:LIST_AT, :] = value[:, columns]
        given[i, LIST_AT:, :] = tile


def kv_pack(key_act, value_act, kv_lists):
    outs = [((len(CHIPS), KV_ROWS, HD), BF16)]
    args = (key_act, value_act, kv_lists)
    scratch = [pltpu.VMEM((8, HD), F32), *(pltpu.VMEM(arg.shape, arg.dtype) for arg in args), pltpu.SemaphoreType.DMA((3,))]
    specs = [pl.BlockSpec(memory_space=pl.ANY)] * 3
    return call(kv_pack_kernel, "kv_pack", specs, outs, scratch, 1, args, limit=60 << 20)[0]


def kv_pair_kernel(key, value, lists, theirs, *rest):
    pairs, rows = rest[:-1], rest[-1]
    me, tile = list_row(lists, rows)
    for i, (chip, pair) in enumerate(zip(CHIPS, pairs)):
        columns = pl.ds(pl.multiple_of((me ^ chip) * HD, HD), HD)
        pair[0, :BLOCK, :] = key[:, columns]
        pair[0, BLOCK:LIST_AT, :] = value[:, columns]
        pair[0, LIST_AT:, :] = tile
        pair[1] = theirs[i]


def kv_pair(key_act, value_act, kv_lists, theirs):
    outs = [((2, KV_ROWS, HD), BF16)] * len(CHIPS)
    args = (key_act, value_act, kv_lists, theirs)
    return call(kv_pair_kernel, "kv_pair", in_vmem(4), outs, [pltpu.VMEM((8, HD), F32)], 0.5, args)


def pair_up_kernel(mine, theirs, *pairs):
    for i, pair in enumerate(pairs):
        pair[0] = mine[i]
        pair[1] = theirs[i]


def pair_up(mine, theirs, after=()):
    outs = [((2, *mine.shape[1:]), mine.dtype)] * mine.shape[0]
    return call(pair_up_kernel, "pair_up", in_vmem(2), outs, [], 0.5, (mine, theirs), after)


def pass_on_kernel(source, target):
    target[...] = source[...]


def pass_on(array, after):
    return call(pass_on_kernel, "pass_on", in_vmem(1), [(array.shape, array.dtype)], [], 0.2, (array,), after)[0]


def kv_sum_kernel(mine, theirs, kept, given):
    for i in range(mine.shape[0]):
        target = given if i % 2 else kept
        target[i // 2] = (mine[i] + theirs[i].astype(F32)).astype(BF16)


def kv_sum(mine, theirs):
    outs = [((mine.shape[0] // 2, *mine.shape[1:]), BF16)] * 2
    return call(kv_sum_kernel, "kv_sum", in_vmem(2), outs, [], 0.5, (mine, theirs))


def qg_pack_kernel(slots, query, grad, out, totals, *rest):
    packed, totals_by_group = rest[:-1], rest[-1]
    me = lax.rem(lax.axis_index("blk"), KVH)
    totals_by_group[...] = jnp.zeros(totals_by_group.shape, F32)
    for g in range(KVH):
        totals_by_group[g, :GROUP, :] = totals[g * GROUP : (g + 1) * GROUP, :]
    head_of = lax.broadcasted_iota(jnp.int32, (8, Q_ROWS), 1) // HD
    picks = jnp.where(head_of == lax.broadcasted_iota(jnp.int32, (8, Q_ROWS), 0), 1.0, 0.0).astype(BF16)
    for message, ks in zip(packed, slots):
        for n, k in enumerate(ks):
            columns = pl.ds(pl.multiple_of((me ^ k) * Q_ROWS, Q_ROWS), Q_ROWS)
            queries, grads = query[:, columns], grad[:, columns]
            for h in range(GROUP):
                message[n, h * BLOCK : (h + 1) * BLOCK, :] = queries[:, h * HD : (h + 1) * HD]
                message[n, Q_ROWS + h * BLOCK : Q_ROWS + (h + 1) * BLOCK, :] = grads[:, h * HD : (h + 1) * HD]
            product = grads.astype(F32) * out[:, columns].astype(F32)
            high = product.astype(BF16)
            low = (product - high.astype(F32)).astype(BF16)
            delta = dot_nt(picks, high) + dot_nt(picks, low)
            extras = jnp.concatenate([totals_by_group[me ^ k], delta], axis=0)
            for i, part in enumerate(three_parts(extras)):
                message[n, X_AT + 16 * i : X_AT + 16 * (i + 1), :] = part


def qg_pack(slots, query_act, grad_out, attn_out, totals, after):
    outs = [((len(ks), QG_ROWS, HD), BF16) for ks in slots]
    scratch = [pltpu.VMEM((KVH, 8, HD), F32)]
    args = (query_act, grad_out, attn_out, totals)
    return call(functools.partial(qg_pack_kernel, slots), "qg_pack", in_vmem(4), outs, scratch, 1, args, after)


def attend_kernel(ks, kind, *refs):
    refs = list(refs)
    opens, joins, closes = kind == "first", kind in ("join", "last"), kind == "last"
    lists = refs.pop(0)
    messages = []
    while len(messages) < len(ks):
        ref = refs.pop(0)
        messages += [ref.at[n] for n in range(ref.shape[0])]
    if opens:
        kv_own, kv_other = [refs.pop(0) for _ in CHIPS], [refs.pop(0) for _ in CHIPS]
    else:
        keys, keys_t, values, sums_in = (refs.pop(0) for _ in range(4))
    if joins:
        earlier = refs.pop(0)
        backs = [refs.pop(0) for _ in ks]
        for n, back in enumerate(backs):
            back[0] = earlier[n]
        query_grads = [back.at[1] for back in backs]
    else:
        back = refs.pop(0)
        query_grads = [back.at[n] for n in range(len(ks))]
    if closes:
        mine, others = [refs.pop(0) for _ in BACK_HALVES], [refs.pop(0) for _ in BACK_HALVES]
    if opens:
        keys, keys_t, values = (refs.pop(0) for _ in range(3))
    sums = refs.pop(0)
    query_sum, probs_held, scores_held = refs
    me, parity = lists[0, OWN_COL] // 2, lists[0, OWN_COL] % 2
    spare = 2 * KVH

    if opens:
        for own, other, chip in zip(kv_own, kv_other, CHIPS):
            for n in range(2):
                at = 2 * (me ^ (chip + n))
                for ref, j in ((own, at + parity), (other, at + 1 - parity)):
                    keys[j] = ref[n, :BLOCK, :]
                    values[j] = ref[n, BLOCK:LIST_AT, :]
                    keys_t[j] = ref[n, :BLOCK, :].T
        zero = jnp.zeros((BLOCK, HD), BF16)
        keys[spare], keys_t[spare], values[spare] = zero, zero, zero
        sums[...] = jnp.zeros(sums.shape, F32)
    else:
        sums[...] = sums_in[...]

    def both(ref, pair, axis):
        return jnp.concatenate([ref[j] for j in pair], axis=axis)

    def produce(n, pair, extras, diagonal):
        totals, deltas = extras
        scores = dot_nt(both(keys, pair, 0), messages[n][:Q_ROWS, :])
        probs = jnp.exp2(scores * (SCALING * math.log2(math.e)) - totals)
        if diagonal:
            at_key = lax.broadcasted_iota(jnp.int32, probs.shape, 0) - BLOCK
            at_query = lax.broadcasted_iota(jnp.int32, probs.shape, 1) % BLOCK
            probs = jnp.where(at_key <= at_query, probs, 0.0)
        grad_probs = dot_nt(both(values, pair, 0), messages[n][Q_ROWS:X_AT, :])
        probs_held[...] = probs.astype(BF16)
        scores_held[...] = (probs * (grad_probs - deltas)).astype(BF16)

    def consume(n, pair):
        probs_low, grad_scores = probs_held[...], scores_held[...]
        value_part = dot_nn(probs_low, messages[n][Q_ROWS:X_AT, :])
        key_part = dot_nn(grad_scores, messages[n][:Q_ROWS, :])
        query_sum[...] += dot_nn(both(keys_t, pair, 1), grad_scores)
        for i, j in enumerate(pair):
            sums[j, :BLOCK, :] += key_part[i * BLOCK : (i + 1) * BLOCK, :]
            sums[j, BLOCK:, :] += value_part[i * BLOCK : (i + 1) * BLOCK, :]

    def finish(n):
        for h in range(GROUP):
            part = query_sum[:, h * BLOCK : (h + 1) * BLOCK].T
            query_grads[n][h * BLOCK : (h + 1) * BLOCK, :] = (part * SCALING).astype(BF16)

    pair = None
    for n, k in enumerate(ks):
        parts = [messages[n][X_AT + 16 * i : X_AT + 16 * (i + 1), :].astype(F32) for i in range(3)]
        rows = parts[0] + parts[1] + parts[2]
        totals = jnp.concatenate([rows[h : h + 1, :] for h in range(GROUP)], axis=1) * math.log2(math.e)
        deltas = jnp.concatenate([rows[8 + h : 9 + h, :] for h in range(GROUP)], axis=1)
        extras = (totals, deltas)
        count = lists[k, COUNT_COL]
        pairs = count // 2
        left = jnp.where(count % 2 == 1, lists[k, jnp.maximum(count - 1, 0)], spare)
        if pair is not None:
            consume(n - 1, pair)
        produce(n, (left, lists[k, OWN_COL]), extras, True)
        if pair is not None:
            finish(n - 1)
        query_sum[...] = jnp.zeros(query_sum.shape, F32)

        def visit(t, held):
            consume(n, held)
            following = (lists[k, 2 * t], lists[k, 2 * t + 1])
            produce(n, following, extras, False)
            return following

        pair = lax.fori_loop(0, pairs, visit, (left, lists[k, OWN_COL]))
    consume(len(ks) - 1, pair)
    finish(len(ks) - 1)

    if closes:
        for half, own, other in zip(BACK_HALVES, mine, others):
            for i, k in enumerate(half):
                at = 2 * (me ^ k)
                own[i, :BLOCK, :] = sums[at + parity, :BLOCK, :] * SCALING
                own[i, BLOCK:, :] = sums[at + parity, BLOCK:, :]
                other[i, :BLOCK, :] = (sums[at + 1 - parity, :BLOCK, :] * SCALING).astype(BF16)
                other[i, BLOCK:, :] = sums[at + 1 - parity, BLOCK:, :].astype(BF16)


def attend(name, kind, ks, lists, messages, state, micros):
    blocks = 2 * KVH + 1
    sums = ((blocks, 2 * BLOCK, HD), F32)
    scratch = []
    if kind in ("join", "last"):
        outs = [((2, Q_ROWS, HD), BF16)] * len(ks)
    else:
        outs = [((len(ks), Q_ROWS, HD), BF16)]
    if kind == "first":
        outs += [((blocks, BLOCK, HD), BF16)] * 3
    if kind == "last":
        outs += [((KVH // 2, 2 * BLOCK, HD), kind) for kind in (F32, F32, BF16, BF16)]
        scratch = [pltpu.VMEM(*sums)]
    else:
        outs += [sums]
    scratch += [pltpu.VMEM((HD, Q_ROWS), F32), pltpu.VMEM((2 * BLOCK, Q_ROWS), BF16), pltpu.VMEM((2 * BLOCK, Q_ROWS), BF16)]
    specs = [pl.BlockSpec(memory_space=pltpu.SMEM)] + in_vmem(len(messages) + len(state))
    kernel = functools.partial(attend_kernel, ks, kind)
    return call(kernel, name, specs, outs, scratch, micros, (lists, *messages, *state))


def query_relay_kernel(own, *refs):
    given = refs[-1]
    given[0] = own[1]
    for i, back in enumerate(refs[:-1]):
        given[i + 1] = back[1]


def query_unpack_kernel(*refs):
    backs, theirs, query_grad, done = refs[: len(CHIPS)], *refs[len(CHIPS) :]
    done[...] = jnp.zeros(done.shape, F32)
    me = lax.rem(lax.axis_index("blk"), KVH)
    for i, chip in enumerate(CHIPS):
        for k, ref, n in ((chip, backs[i], 0), (chip + 1, theirs, i)):
            for h in range(GROUP):
                columns = pl.ds(pl.multiple_of(((me ^ k) * GROUP + h) * HD, HD), HD)
                query_grad[:, columns] = ref[n, h * BLOCK : (h + 1) * BLOCK, :]


def kv_unpack_kernel(*refs):
    key_grad, value_grad = refs[len(CHIPS) :]
    me = lax.rem(lax.axis_index("blk"), KVH)
    for i, chip in enumerate(CHIPS):
        for n in range(2):
            columns = pl.ds(pl.multiple_of((me ^ (chip + n)) * HD, HD), HD)
            key_grad[:, columns] = refs[i][n, :BLOCK, :]
            value_grad[:, columns] = refs[i][n, BLOCK:, :]


CHIPS = (0, 2, 4, 6)
CHIPS = (0, 2, 4, 6)
VISITS = (("first", (0, 1)), ("more", (6, 7)), ("more", (2, 4)), ("last", (3, 5)))
EXPECTED = (0.5, 0.5, 0.5, 6)
BACK_HALVES = ((6, 7, 2, 3), (4, 5, 0, 1))


def by_trees(query_act, key_act, value_act, attn_out, grad_out, log_sum, kv_lists):
    size = lax.axis_size("blk")

    def exchanged(array, k):
        return lax.ppermute(array, "blk", [(i, i ^ k) for i in range(size)])

    def swapped(array):
        return lax.ppermute(array, "head", [(0, 1), (1, 0)])

    given = kv_pack(key_act, value_act, kv_lists)
    paired = kv_pair(key_act, value_act, kv_lists, exchanged(given, 1))
    kv_own = [paired[0], *(exchanged(part, chip) for part, chip in zip(paired[1:], CHIPS[1:]))]
    kv_other = [swapped(part) for part in kv_own]
    lists = jnp.concatenate([part[:, LIST_AT, : OWN_COL + 1] for part in kv_own]).astype(jnp.int32)

    qg = (query_act, grad_out, attn_out, log_sum.T)
    own, far, given = qg_pack(((0,), (6,), (1, 7)), *qg, (paired[1],))
    beside = exchanged(given, 1)
    far = pair_up(far, beside[1:], (*kv_own[1:], kv_other[0]))[0]
    here = [[own, beside[:1]], [exchanged(far, 6)]]
    for ks, after in (((2, 4), kv_other[2]), ((3, 5), kv_other[3])):
        sent = qg_pack([(k,) for k in ks], *qg, (after,))
        here.append([exchanged(message, k) for k, message in zip(ks, sent)])

    state, grads = (*kv_own, *kv_other), []
    for i, (kind, ks) in enumerate(VISITS):
        if kind == "last":
            state = (*state, grads[-1])
        results = attend(f"attend_{i}", kind, ks, lists, here[i], state, EXPECTED[i])
        grads.append(results[0])
        state = tuple(results[1:]) if kind == "first" else (*state[:3], results[-1])
    far_back = exchanged(grads[1], 6)
    backs = [exchanged(results[0], 2), exchanged(results[1], 4), far_back]
    others = (pass_on(results[4], (far_back,)), results[5])
    theirs = [swapped(other) for other in others]
    sums = [kv_sum(mine, other) for mine, other in zip(results[2:4], theirs)]
    kv_back, order = {}, [theirs[1]]
    for half, (kept, given) in zip(BACK_HALVES, sums):
        paired = pair_up(kept, exchanged(given, 1), order[:1])
        order.append(paired[0])
        kv_back.update((chip, exchanged(pair, chip) if chip else pair) for chip, pair in zip(half[::2], paired))
    outs = [((4, Q_ROWS, HD), BF16)]
    given = call(query_relay_kernel, "query_relay", in_vmem(4), outs, [], 0.5, (grads[0], *backs), order[1:2])[0]
    args = (grads[0], *backs, exchanged(given, 1))
    outs = [((BLOCK, QH * HD), BF16), ((8, HD), F32)]
    grad_query, done = call(query_unpack_kernel, "query_unpack", in_vmem(5), outs, [], 1, args)
    outs = [((BLOCK, KVH * HD), BF16)] * 2
    grad_key, grad_value = call(kv_unpack_kernel, "kv_unpack", in_vmem(4), outs, [], 1, [kv_back[chip] for chip in CHIPS], (done,))
    return grad_query, grad_key, grad_value


def passed_along(array, axis, by):
    size = lax.axis_size(axis)
    pairs = [(i, i + by) for i in range(size) if 0 <= i + by < size]
    return lax.ppermute(array, axis, pairs)


def shifted(array, axis, by):
    size = lax.axis_size(axis)
    return lax.ppermute(array, axis, [(i, (i + by) % size) for i in range(size)])


def head_delta(grad_rows, out_rows, heads):
    count = grad_rows.shape[0]
    return jnp.einsum(
        "thd,thd->th",
        grad_rows.reshape(count, heads, HD),
        out_rows.reshape(count, heads, HD),
        preferred_element_type=jnp.float32,
    )


def by_ring(query_act, key_act, value_act, attn_out, grad_out, log_sum, kv_lists):
    head_count = lax.axis_size("head")
    blk_count = lax.axis_size("blk")
    sent_delta = head_delta(grad_out, attn_out, QH)
    query_rows, key_rows, value_rows, grad_rows, total_rows, delta_rows = (
        lax.all_to_all(
            query_act.astype(jnp.float32), "head", split_axis=1, concat_axis=0, tiled=True
        ).astype(query_act.dtype),
        lax.all_to_all(
            key_act.astype(jnp.float32), "head", split_axis=1, concat_axis=0, tiled=True
        ).astype(key_act.dtype),
        lax.all_to_all(
            value_act.astype(jnp.float32), "head", split_axis=1, concat_axis=0, tiled=True
        ).astype(value_act.dtype),
        lax.all_to_all(
            grad_out.astype(jnp.float32), "head", split_axis=1, concat_axis=0, tiled=True
        ).astype(grad_out.dtype),
        lax.all_to_all(log_sum, "head", split_axis=1, concat_axis=0, tiled=True),
        lax.all_to_all(sent_delta, "head", split_axis=1, concat_axis=0, tiled=True),
    )
    tokens = query_rows.shape[0]
    local_heads = KVH // head_count
    group_size = QH // KVH
    blocks_dev = tokens // BLOCK
    scaling = HD ** (-0.5)
    queries = query_rows.reshape(tokens, local_heads, group_size, HD)
    out_grads = grad_rows.reshape(tokens, local_heads, group_size, HD)
    row_totals = total_rows.reshape(tokens, local_heads, group_size).transpose(1, 2, 0)[
        :, :, :, None
    ]
    row_deltas = delta_rows.reshape(tokens, local_heads, group_size).transpose(1, 2, 0)[
        :, :, :, None
    ]
    position = lax.axis_index("blk")
    query_pos = position * tokens + jnp.arange(tokens, dtype=jnp.int32)

    def block_mask(rotation):
        source = (position - rotation) % blk_count
        key_ids = source * blocks_dev + jnp.arange(blocks_dev, dtype=jnp.int32)
        listed = jnp.any(kv_lists[:, :, None] == key_ids[None, None, :], axis=1)
        key_pos = source * tokens + jnp.arange(tokens, dtype=jnp.int32)
        return (listed, key_pos)

    def attend(kv_pair, key_sums, query_grad, listed, key_pos):
        visible = jnp.repeat(jnp.repeat(listed, BLOCK, axis=0), BLOCK, axis=1) & (
            key_pos[None, :] <= query_pos[:, None]
        )
        key_block = kv_pair[0].reshape(tokens, local_heads, HD)
        value_block = kv_pair[1].reshape(tokens, local_heads, HD)
        scores = (
            jnp.einsum("tkgd,skd->kgts", queries, key_block, preferred_element_type=jnp.float32)
            * scaling
        )
        weights = jnp.where(visible, jnp.exp(scores - row_totals), 0.0)
        grad_probs = jnp.einsum(
            "tkgd,skd->kgts", out_grads, value_block, preferred_element_type=jnp.float32
        )
        grad_scores = (weights * (grad_probs - row_deltas)).astype(jnp.bfloat16)
        probs_low = weights.astype(jnp.bfloat16)
        value_part = jnp.einsum(
            "kgts,tkgd->skd", probs_low, out_grads, preferred_element_type=jnp.float32
        )
        key_part = (
            jnp.einsum("kgts,tkgd->skd", grad_scores, queries, preferred_element_type=jnp.float32)
            * scaling
        )
        query_part = (
            jnp.einsum("kgts,skd->tkgd", grad_scores, key_block, preferred_element_type=jnp.float32)
            * scaling
        )
        added = jnp.stack(
            [
                key_part.reshape(tokens, local_heads * HD),
                value_part.reshape(tokens, local_heads * HD),
            ]
        )
        return (key_sums + added, query_grad + query_part)

    def visit(rotation, kv_pair, key_sums, query_grad):
        listed, key_pos = block_mask(rotation)
        return attend(kv_pair, key_sums, query_grad, listed, key_pos)

    kv_pair = jnp.stack([key_rows, value_rows])
    empty_sums = jnp.zeros((2, tokens, local_heads * HD), jnp.float32)
    empty_grad = jnp.zeros((tokens, local_heads, group_size, HD), jnp.float32)

    def advance(rotation, carried):
        kv_here, key_sums, query_grad = carried
        arrived = passed_along(kv_here, "blk", 1)
        key_sums, query_grad = visit(rotation, kv_here, key_sums, query_grad)
        key_sums = shifted(key_sums, "blk", 1)
        return (arrived, key_sums, query_grad)

    kv_here, key_sums, query_grad = lax.fori_loop(
        0, blk_count - 1, advance, (kv_pair, empty_sums, empty_grad)
    )
    key_sums, query_grad = visit(blk_count - 1, kv_here, key_sums, query_grad)
    key_sums = shifted(key_sums.astype(jnp.bfloat16), "blk", 1 - blk_count).astype(key_sums.dtype)
    query_low = query_grad.reshape(tokens, local_heads * group_size * HD).astype(jnp.bfloat16)
    key_low = key_sums[0].astype(jnp.bfloat16)
    value_low = key_sums[1].astype(jnp.bfloat16)
    grad_query, grad_key, grad_value = (
        lax.all_to_all(query_low, "head", split_axis=0, concat_axis=1, tiled=True),
        lax.all_to_all(key_low, "head", split_axis=0, concat_axis=1, tiled=True),
        lax.all_to_all(value_low, "head", split_axis=0, concat_axis=1, tiled=True),
    )
    return (grad_query, grad_key, grad_value)


def local(query_act, *others):
    head_count = lax.axis_size("head")
    blk_count = lax.axis_size("blk")
    if query_act.shape[0] == BLOCK and head_count == 2 and blk_count == 2 * KVH and blk_count * head_count == TREE_B:
        return by_trees(query_act, *others)
    return by_ring(query_act, *others)


def solution(mesh):
    rows = P(("blk", "head"), None)
    return jax.shard_map(
        local,
        mesh=mesh,
        in_specs=(rows,) * 6 + (P("blk", None),),
        out_specs=(rows,) * 3,
        check_vma=False,
    )
```

```python
import functools
import math

import jax
import jax.numpy as jnp
from jax import lax
from jax.experimental import pallas as pl
from jax.experimental.pallas import tpu as pltpu
from jax.sharding import PartitionSpec as P

QH = 40
KVH = 8
HD = 128
BLOCK = 128
TREE_B = 32
GROUP = QH // KVH
SCALING = HD ** (-0.5)
F32 = jnp.float32
BF16 = jnp.bfloat16

Q_ROWS = GROUP * BLOCK
LIST_AT = 2 * BLOCK
KV_ROWS = LIST_AT + 16
X_AT = 2 * Q_ROWS
QG_ROWS = X_AT + 48
COUNT_COL = TREE_B
OWN_COL = TREE_B + 1
VMEM_LIMIT = 14 << 20


def dot_nt(a, b):
    return lax.dot_general(a, b, (((1,), (1,)), ((), ())), preferred_element_type=F32)


def dot_nn(a, b):
    return lax.dot_general(a, b, (((1,), (0,)), ((), ())), preferred_element_type=F32)


def three_parts(array):
    high = array.astype(BF16)
    rest = array - high.astype(F32)
    middle = rest.astype(BF16)
    return high, middle, (rest - middle.astype(F32)).astype(BF16)


def in_vmem(count):
    return [pl.BlockSpec(memory_space=pltpu.VMEM)] * count


def call(kernel, name, in_specs, outs, scratch, micros, args, after=(), limit=VMEM_LIMIT):
    given = len(args)

    def body(*refs):
        kernel(*refs[:given], *refs[given + len(after) :])

    return pl.pallas_call(
        body,
        name=name,
        in_specs=[*in_specs, *[pl.BlockSpec(memory_space=pl.ANY)] * len(after)],
        out_specs=in_vmem(len(outs)),
        out_shape=[jax.ShapeDtypeStruct(*out) for out in outs],
        scratch_shapes=scratch,
        cost_estimate=pl.CostEstimate(flops=int(micros * 1e9), bytes_accessed=int(micros * 3e6), transcendentals=0),
        compiler_params=pltpu.CompilerParams(vmem_limit_bytes=limit),
    )(*args, *after)


def list_row(lists, rows):
    position, parity = lax.axis_index("blk"), lax.axis_index("head")
    me = lax.rem(position, KVH)
    first = (position - me) * 2
    rows[...] = jnp.full(rows.shape, -1.0, F32)
    rows[:2, :TREE_B] = lists[...].astype(F32)
    row = jnp.where(parity == 0, rows[0:1, :], rows[1:2, :])
    seen = row >= 0
    count = jnp.sum(jnp.where(seen, 1.0, 0.0)) - 1.0
    lane = lax.broadcasted_iota(jnp.int32, row.shape, 1)
    row = jnp.where(seen, row - first.astype(F32), -1.0)
    row = jnp.where(lane == COUNT_COL, count, row)
    row = jnp.where(lane == OWN_COL, (2 * me + parity).astype(F32), row)
    return me, jnp.broadcast_to(row, (KV_ROWS - LIST_AT, HD)).astype(BF16)


def kv_pack_kernel(key_in, value_in, lists_in, given, rows, key, value, lists, arrived):
    copies = [
        pltpu.make_async_copy(source, target, arrived.at[i])
        for i, (source, target) in enumerate(((lists_in, lists), (key_in, key), (value_in, value)))
    ]
    for copy in copies:
        copy.start()
    for copy in copies:
        copy.wait()
    me, tile = list_row(lists, rows)
    for i, chip in enumerate(CHIPS):
        columns = pl.ds(pl.multiple_of((me ^ (chip + 1)) * HD, HD), HD)
        given[i, :BLOCK, :] = key[:, columns]
        given[i, BLOCK:LIST_AT, :] = value[:, columns]
        given[i, LIST_AT:, :] = tile


def kv_pack(key_act, value_act, kv_lists):
    outs = [((len(CHIPS), KV_ROWS, HD), BF16)]
    args = (key_act, value_act, kv_lists)
    scratch = [pltpu.VMEM((8, HD), F32), *(pltpu.VMEM(arg.shape, arg.dtype) for arg in args), pltpu.SemaphoreType.DMA((3,))]
    specs = [pl.BlockSpec(memory_space=pl.ANY)] * 3
    return call(kv_pack_kernel, "kv_pack", specs, outs, scratch, 1, args, limit=60 << 20)[0]


def kv_pair_kernel(key, value, lists, theirs, *rest):
    pairs, rows = rest[:-1], rest[-1]
    me, tile = list_row(lists, rows)
    for i, (chip, pair) in enumerate(zip(CHIPS, pairs)):
        columns = pl.ds(pl.multiple_of((me ^ chip) * HD, HD), HD)
        pair[0, :BLOCK, :] = key[:, columns]
        pair[0, BLOCK:LIST_AT, :] = value[:, columns]
        pair[0, LIST_AT:, :] = tile
        pair[1] = theirs[i]


def kv_pair(key_act, value_act, kv_lists, theirs):
    outs = [((2, KV_ROWS, HD), BF16)] * len(CHIPS)
    args = (key_act, value_act, kv_lists, theirs)
    return call(kv_pair_kernel, "kv_pair", in_vmem(4), outs, [pltpu.VMEM((8, HD), F32)], 0.5, args)


def pair_up_kernel(mine, theirs, *pairs):
    for i, pair in enumerate(pairs):
        pair[0] = mine[i]
        pair[1] = theirs[i]


def pair_up(mine, theirs, after=()):
    outs = [((2, *mine.shape[1:]), mine.dtype)] * mine.shape[0]
    return call(pair_up_kernel, "pair_up", in_vmem(2), outs, [], 0.5, (mine, theirs), after)


def pass_on_kernel(source, target):
    target[...] = source[...]


def pass_on(array, after):
    return call(pass_on_kernel, "pass_on", in_vmem(1), [(array.shape, array.dtype)], [], 0.2, (array,), after)[0]


def kv_sum_kernel(mine, theirs, total):
    for i in range(mine.shape[0]):
        total[i] = (mine[i] + theirs[i].astype(F32)).astype(BF16)


def kv_sum(mine, theirs):
    return call(kv_sum_kernel, "kv_sum", in_vmem(2), [(mine.shape, BF16)], [], 0.5, (mine, theirs))[0]


def qg_pack_kernel(slots, query, grad, out, totals, *rest):
    packed, totals_by_group = rest[:-1], rest[-1]
    me = lax.rem(lax.axis_index("blk"), KVH)
    totals_by_group[...] = jnp.zeros(totals_by_group.shape, F32)
    for g in range(KVH):
        totals_by_group[g, :GROUP, :] = totals[g * GROUP : (g + 1) * GROUP, :]
    head_of = lax.broadcasted_iota(jnp.int32, (8, Q_ROWS), 1) // HD
    picks = jnp.where(head_of == lax.broadcasted_iota(jnp.int32, (8, Q_ROWS), 0), 1.0, 0.0).astype(BF16)
    for message, ks in zip(packed, slots):
        for n, k in enumerate(ks):
            columns = pl.ds(pl.multiple_of((me ^ k) * Q_ROWS, Q_ROWS), Q_ROWS)
            queries, grads = query[:, columns], grad[:, columns]
            for h in range(GROUP):
                message[n, h * BLOCK : (h + 1) * BLOCK, :] = queries[:, h * HD : (h + 1) * HD]
                message[n, Q_ROWS + h * BLOCK : Q_ROWS + (h + 1) * BLOCK, :] = grads[:, h * HD : (h + 1) * HD]
            product = grads.astype(F32) * out[:, columns].astype(F32)
            high = product.astype(BF16)
            low = (product - high.astype(F32)).astype(BF16)
            delta = dot_nt(picks, high) + dot_nt(picks, low)
            extras = jnp.concatenate([totals_by_group[me ^ k], delta], axis=0)
            for i, part in enumerate(three_parts(extras)):
                message[n, X_AT + 16 * i : X_AT + 16 * (i + 1), :] = part


def qg_pack(slots, query_act, grad_out, attn_out, totals, after):
    outs = [((len(ks), QG_ROWS, HD), BF16) for ks in slots]
    scratch = [pltpu.VMEM((KVH, 8, HD), F32)]
    args = (query_act, grad_out, attn_out, totals)
    return call(functools.partial(qg_pack_kernel, slots), "qg_pack", in_vmem(4), outs, scratch, 1, args, after)


def attend_kernel(ks, kind, *refs):
    refs = list(refs)
    opens, joins, closes = kind == "first", kind in ("join", "last"), kind == "last"
    lists = refs.pop(0)
    messages = []
    while len(messages) < len(ks):
        ref = refs.pop(0)
        messages += [ref.at[n] for n in range(ref.shape[0])]
    if opens:
        kv_own, kv_other = [refs.pop(0) for _ in CHIPS], [refs.pop(0) for _ in CHIPS]
    else:
        keys, keys_t, values, sums_in = (refs.pop(0) for _ in range(4))
    if joins:
        earlier = refs.pop(0)
        backs = [refs.pop(0) for _ in ks]
        for n, back in enumerate(backs):
            back[0] = earlier[n]
        query_grads = [back.at[1] for back in backs]
    else:
        back = refs.pop(0)
        query_grads = [back.at[n] for n in range(len(ks))]
    if closes:
        mine, others = [refs.pop(0) for _ in BACK_HALVES], [refs.pop(0) for _ in BACK_HALVES]
    if opens:
        keys, keys_t, values = (refs.pop(0) for _ in range(3))
    sums = refs.pop(0)
    query_sum, probs_held, scores_held = refs
    me, parity = lists[0, OWN_COL] // 2, lists[0, OWN_COL] % 2
    spare = 2 * KVH

    if opens:
        for own, other, chip in zip(kv_own, kv_other, CHIPS):
            for n in range(2):
                at = 2 * (me ^ (chip + n))
                for ref, j in ((own, at + parity), (other, at + 1 - parity)):
                    keys[j] = ref[n, :BLOCK, :]
                    values[j] = ref[n, BLOCK:LIST_AT, :]
                    keys_t[j] = ref[n, :BLOCK, :].T
        zero = jnp.zeros((BLOCK, HD), BF16)
        keys[spare], keys_t[spare], values[spare] = zero, zero, zero
        sums[...] = jnp.zeros(sums.shape, F32)
    else:
        sums[...] = sums_in[...]

    def both(ref, pair, axis):
        return jnp.concatenate([ref[j] for j in pair], axis=axis)

    def produce(n, pair, extras, diagonal):
        totals, deltas = extras
        scores = dot_nt(both(keys, pair, 0), messages[n][:Q_ROWS, :])
        probs = jnp.exp2(scores * (SCALING * math.log2(math.e)) - totals)
        if diagonal:
            at_key = lax.broadcasted_iota(jnp.int32, probs.shape, 0) - BLOCK
            at_query = lax.broadcasted_iota(jnp.int32, probs.shape, 1) % BLOCK
            probs = jnp.where(at_key <= at_query, probs, 0.0)
        grad_probs = dot_nt(both(values, pair, 0), messages[n][Q_ROWS:X_AT, :])
        probs_held[...] = probs.astype(BF16)
        scores_held[...] = (probs * (grad_probs - deltas)).astype(BF16)

    def consume(n, pair):
        probs_low, grad_scores = probs_held[...], scores_held[...]
        value_part = dot_nn(probs_low, messages[n][Q_ROWS:X_AT, :])
        key_part = dot_nn(grad_scores, messages[n][:Q_ROWS, :])
        query_sum[...] += dot_nn(both(keys_t, pair, 1), grad_scores)
        for i, j in enumerate(pair):
            sums[j, :BLOCK, :] += key_part[i * BLOCK : (i + 1) * BLOCK, :]
            sums[j, BLOCK:, :] += value_part[i * BLOCK : (i + 1) * BLOCK, :]

    def finish(n):
        for h in range(GROUP):
            part = query_sum[:, h * BLOCK : (h + 1) * BLOCK].T
            query_grads[n][h * BLOCK : (h + 1) * BLOCK, :] = (part * SCALING).astype(BF16)

    pair = None
    for n, k in enumerate(ks):
        parts = [messages[n][X_AT + 16 * i : X_AT + 16 * (i + 1), :].astype(F32) for i in range(3)]
        rows = parts[0] + parts[1] + parts[2]
        totals = jnp.concatenate([rows[h : h + 1, :] for h in range(GROUP)], axis=1) * math.log2(math.e)
        deltas = jnp.concatenate([rows[8 + h : 9 + h, :] for h in range(GROUP)], axis=1)
        extras = (totals, deltas)
        count = lists[k, COUNT_COL]
        pairs = count // 2
        left = jnp.where(count % 2 == 1, lists[k, jnp.maximum(count - 1, 0)], spare)
        if pair is not None:
            consume(n - 1, pair)
        produce(n, (left, lists[k, OWN_COL]), extras, True)
        if pair is not None:
            finish(n - 1)
        query_sum[...] = jnp.zeros(query_sum.shape, F32)

        def visit(t, held):
            consume(n, held)
            following = (lists[k, 2 * t], lists[k, 2 * t + 1])
            produce(n, following, extras, False)
            return following

        pair = lax.fori_loop(0, pairs, visit, (left, lists[k, OWN_COL]))
    consume(len(ks) - 1, pair)
    finish(len(ks) - 1)

    if closes:
        for half, own, other in zip(BACK_HALVES, mine, others):
            for i, k in enumerate(half):
                at = 2 * (me ^ k)
                own[i, :BLOCK, :] = sums[at + parity, :BLOCK, :] * SCALING
                own[i, BLOCK:, :] = sums[at + parity, BLOCK:, :]
                other[i, :BLOCK, :] = (sums[at + 1 - parity, :BLOCK, :] * SCALING).astype(BF16)
                other[i, BLOCK:, :] = sums[at + 1 - parity, BLOCK:, :].astype(BF16)


def attend(name, kind, ks, lists, messages, state, micros):
    blocks = 2 * KVH + 1
    sums = ((blocks, 2 * BLOCK, HD), F32)
    scratch = []
    if kind in ("join", "last"):
        outs = [((2, Q_ROWS, HD), BF16)] * len(ks)
    else:
        outs = [((len(ks), Q_ROWS, HD), BF16)]
    if kind == "first":
        outs += [((blocks, BLOCK, HD), BF16)] * 3
    if kind == "last":
        outs += [((KVH // 2, 2 * BLOCK, HD), kind) for kind in (F32, F32, BF16, BF16)]
        scratch = [pltpu.VMEM(*sums)]
    else:
        outs += [sums]
    scratch += [pltpu.VMEM((HD, Q_ROWS), F32), pltpu.VMEM((2 * BLOCK, Q_ROWS), BF16), pltpu.VMEM((2 * BLOCK, Q_ROWS), BF16)]
    specs = [pl.BlockSpec(memory_space=pltpu.SMEM)] + in_vmem(len(messages) + len(state))
    kernel = functools.partial(attend_kernel, ks, kind)
    return call(kernel, name, specs, outs, scratch, micros, (lists, *messages, *state))


def query_relay_kernel(own, *refs):
    given = refs[-1]
    given[0] = own[1]
    for i, back in enumerate(refs[:-1]):
        given[i + 1] = back[1]


def query_unpack_kernel(*refs):
    backs, theirs, query_grad, done = refs[: len(CHIPS)], *refs[len(CHIPS) :]
    done[...] = jnp.zeros(done.shape, F32)
    me = lax.rem(lax.axis_index("blk"), KVH)
    for i, chip in enumerate(CHIPS):
        for k, ref, n in ((chip, backs[i], 0), (chip + 1, theirs, i)):
            for h in range(GROUP):
                columns = pl.ds(pl.multiple_of(((me ^ k) * GROUP + h) * HD, HD), HD)
                query_grad[:, columns] = ref[n, h * BLOCK : (h + 1) * BLOCK, :]


def kv_unpack_kernel(*refs):
    key_grad, value_grad = refs[len(CHIPS) :]
    me = lax.rem(lax.axis_index("blk"), KVH)
    for i, chip in enumerate(CHIPS):
        for n in range(2):
            columns = pl.ds(pl.multiple_of((me ^ (chip + n)) * HD, HD), HD)
            key_grad[:, columns] = refs[i][n, :BLOCK, :]
            value_grad[:, columns] = refs[i][n, BLOCK:, :]


CHIPS = (0, 2, 4, 6)
CHIPS = (0, 2, 4, 6)
VISITS = (("first", (0, 1)), ("more", (6, 7)), ("more", (2, 4)), ("last", (3, 5)))
EXPECTED = (0.5, 0.5, 0.5, 6)
BACK_HALVES = ((1, 3, 5, 7), CHIPS)


def by_trees(query_act, key_act, value_act, attn_out, grad_out, log_sum, kv_lists):
    size = lax.axis_size("blk")

    def exchanged(array, k):
        return lax.ppermute(array, "blk", [(i, i ^ k) for i in range(size)])

    def swapped(array):
        return lax.ppermute(array, "head", [(0, 1), (1, 0)])

    given = kv_pack(key_act, value_act, kv_lists)
    paired = kv_pair(key_act, value_act, kv_lists, exchanged(given, 1))
    kv_own = [paired[0], *(exchanged(part, chip) for part, chip in zip(paired[1:], CHIPS[1:]))]
    kv_other = [swapped(part) for part in kv_own]
    lists = jnp.concatenate([part[:, LIST_AT, : OWN_COL + 1] for part in kv_own]).astype(jnp.int32)

    qg = (query_act, grad_out, attn_out, log_sum.T)
    beside = exchanged(qg_pack(((1, 7),), *qg, (paired[1],))[0], 1)
    own, far = qg_pack(((0,), (6,)), *qg, (kv_other[0],))
    far = pair_up(far, beside[1:], (*kv_own[1:], kv_other[0]))[0]
    here = [[own, beside[:1]], [exchanged(far, 6)]]
    for ks, after in (((2, 4), kv_other[2]), ((3, 5), kv_other[3])):
        sent = qg_pack([(k,) for k in ks], *qg, (after,))
        here.append([exchanged(message, k) for k, message in zip(ks, sent)])

    state, grads = (*kv_own, *kv_other), []
    for i, (kind, ks) in enumerate(VISITS):
        if kind == "last":
            state = (*state, grads[-1])
        results = attend(f"attend_{i}", kind, ks, lists, here[i], state, EXPECTED[i])
        grads.append(results[0])
        state = tuple(results[1:]) if kind == "first" else (*state[:3], results[-1])
    far_back = exchanged(grads[1], 6)
    backs = [exchanged(results[0], 2), exchanged(results[1], 4), far_back]
    others = (pass_on(results[4], (far_back,)), results[5])
    theirs = [swapped(other) for other in others]
    given, kept = [kv_sum(mine, other) for mine, other in zip(results[2:4], theirs)]
    paired = pair_up(kept, exchanged(given, 1))
    kv_back = [paired[0], *(exchanged(pair, chip) for pair, chip in zip(paired[1:], CHIPS[1:]))]
    outs = [((4, Q_ROWS, HD), BF16)]
    given = call(query_relay_kernel, "query_relay", in_vmem(4), outs, [], 0.5, (grads[0], *backs), paired[:1])[0]
    args = (grads[0], *backs, exchanged(given, 1))
    outs = [((BLOCK, QH * HD), BF16), ((8, HD), F32)]
    grad_query, done = call(query_unpack_kernel, "query_unpack", in_vmem(5), outs, [], 1, args)
    outs = [((BLOCK, KVH * HD), BF16)] * 2
    grad_key, grad_value = call(kv_unpack_kernel, "kv_unpack", in_vmem(4), outs, [], 1, kv_back, (done,))
    return grad_query, grad_key, grad_value


def passed_along(array, axis, by):
    size = lax.axis_size(axis)
    pairs = [(i, i + by) for i in range(size) if 0 <= i + by < size]
    return lax.ppermute(array, axis, pairs)


def shifted(array, axis, by):
    size = lax.axis_size(axis)
    return lax.ppermute(array, axis, [(i, (i + by) % size) for i in range(size)])


def head_delta(grad_rows, out_rows, heads):
    count = grad_rows.shape[0]
    return jnp.einsum(
        "thd,thd->th",
        grad_rows.reshape(count, heads, HD),
        out_rows.reshape(count, heads, HD),
        preferred_element_type=jnp.float32,
    )


def by_ring(query_act, key_act, value_act, attn_out, grad_out, log_sum, kv_lists):
    head_count = lax.axis_size("head")
    blk_count = lax.axis_size("blk")
    sent_delta = head_delta(grad_out, attn_out, QH)
    query_rows, key_rows, value_rows, grad_rows, total_rows, delta_rows = (
        lax.all_to_all(
            query_act.astype(jnp.float32), "head", split_axis=1, concat_axis=0, tiled=True
        ).astype(query_act.dtype),
        lax.all_to_all(
            key_act.astype(jnp.float32), "head", split_axis=1, concat_axis=0, tiled=True
        ).astype(key_act.dtype),
        lax.all_to_all(
            value_act.astype(jnp.float32), "head", split_axis=1, concat_axis=0, tiled=True
        ).astype(value_act.dtype),
        lax.all_to_all(
            grad_out.astype(jnp.float32), "head", split_axis=1, concat_axis=0, tiled=True
        ).astype(grad_out.dtype),
        lax.all_to_all(log_sum, "head", split_axis=1, concat_axis=0, tiled=True),
        lax.all_to_all(sent_delta, "head", split_axis=1, concat_axis=0, tiled=True),
    )
    tokens = query_rows.shape[0]
    local_heads = KVH // head_count
    group_size = QH // KVH
    blocks_dev = tokens // BLOCK
    scaling = HD ** (-0.5)
    queries = query_rows.reshape(tokens, local_heads, group_size, HD)
    out_grads = grad_rows.reshape(tokens, local_heads, group_size, HD)
    row_totals = total_rows.reshape(tokens, local_heads, group_size).transpose(1, 2, 0)[
        :, :, :, None
    ]
    row_deltas = delta_rows.reshape(tokens, local_heads, group_size).transpose(1, 2, 0)[
        :, :, :, None
    ]
    position = lax.axis_index("blk")
    query_pos = position * tokens + jnp.arange(tokens, dtype=jnp.int32)

    def block_mask(rotation):
        source = (position - rotation) % blk_count
        key_ids = source * blocks_dev + jnp.arange(blocks_dev, dtype=jnp.int32)
        listed = jnp.any(kv_lists[:, :, None] == key_ids[None, None, :], axis=1)
        key_pos = source * tokens + jnp.arange(tokens, dtype=jnp.int32)
        return (listed, key_pos)

    def attend(kv_pair, key_sums, query_grad, listed, key_pos):
        visible = jnp.repeat(jnp.repeat(listed, BLOCK, axis=0), BLOCK, axis=1) & (
            key_pos[None, :] <= query_pos[:, None]
        )
        key_block = kv_pair[0].reshape(tokens, local_heads, HD)
        value_block = kv_pair[1].reshape(tokens, local_heads, HD)
        scores = (
            jnp.einsum("tkgd,skd->kgts", queries, key_block, preferred_element_type=jnp.float32)
            * scaling
        )
        weights = jnp.where(visible, jnp.exp(scores - row_totals), 0.0)
        grad_probs = jnp.einsum(
            "tkgd,skd->kgts", out_grads, value_block, preferred_element_type=jnp.float32
        )
        grad_scores = (weights * (grad_probs - row_deltas)).astype(jnp.bfloat16)
        probs_low = weights.astype(jnp.bfloat16)
        value_part = jnp.einsum(
            "kgts,tkgd->skd", probs_low, out_grads, preferred_element_type=jnp.float32
        )
        key_part = (
            jnp.einsum("kgts,tkgd->skd", grad_scores, queries, preferred_element_type=jnp.float32)
            * scaling
        )
        query_part = (
            jnp.einsum("kgts,skd->tkgd", grad_scores, key_block, preferred_element_type=jnp.float32)
            * scaling
        )
        added = jnp.stack(
            [
                key_part.reshape(tokens, local_heads * HD),
                value_part.reshape(tokens, local_heads * HD),
            ]
        )
        return (key_sums + added, query_grad + query_part)

    def visit(rotation, kv_pair, key_sums, query_grad):
        listed, key_pos = block_mask(rotation)
        return attend(kv_pair, key_sums, query_grad, listed, key_pos)

    kv_pair = jnp.stack([key_rows, value_rows])
    empty_sums = jnp.zeros((2, tokens, local_heads * HD), jnp.float32)
    empty_grad = jnp.zeros((tokens, local_heads, group_size, HD), jnp.float32)

    def advance(rotation, carried):
        kv_here, key_sums, query_grad = carried
        arrived = passed_along(kv_here, "blk", 1)
        key_sums, query_grad = visit(rotation, kv_here, key_sums, query_grad)
        key_sums = shifted(key_sums, "blk", 1)
        return (arrived, key_sums, query_grad)

    kv_here, key_sums, query_grad = lax.fori_loop(
        0, blk_count - 1, advance, (kv_pair, empty_sums, empty_grad)
    )
    key_sums, query_grad = visit(blk_count - 1, kv_here, key_sums, query_grad)
    key_sums = shifted(key_sums.astype(jnp.bfloat16), "blk", 1 - blk_count).astype(key_sums.dtype)
    query_low = query_grad.reshape(tokens, local_heads * group_size * HD).astype(jnp.bfloat16)
    key_low = key_sums[0].astype(jnp.bfloat16)
    value_low = key_sums[1].astype(jnp.bfloat16)
    grad_query, grad_key, grad_value = (
        lax.all_to_all(query_low, "head", split_axis=0, concat_axis=1, tiled=True),
        lax.all_to_all(key_low, "head", split_axis=0, concat_axis=1, tiled=True),
        lax.all_to_all(value_low, "head", split_axis=0, concat_axis=1, tiled=True),
    )
    return (grad_query, grad_key, grad_value)


def local(query_act, *others):
    head_count = lax.axis_size("head")
    blk_count = lax.axis_size("blk")
    if query_act.shape[0] == BLOCK and head_count == 2 and blk_count == 2 * KVH and blk_count * head_count == TREE_B:
        return by_trees(query_act, *others)
    return by_ring(query_act, *others)


def solution(mesh):
    rows = P(("blk", "head"), None)
    return jax.shard_map(
        local,
        mesh=mesh,
        in_specs=(rows,) * 6 + (P("blk", None),),
        out_specs=(rows,) * 3,
        check_vma=False,
    )
```

```python
import functools
import math

import jax
import jax.numpy as jnp
from jax import lax
from jax.experimental import pallas as pl
from jax.experimental.pallas import tpu as pltpu
from jax.sharding import PartitionSpec as P

QH = 40
KVH = 8
HD = 128
BLOCK = 128
TREE_B = 32
GROUP = QH // KVH
SCALING = HD ** (-0.5)
F32 = jnp.float32
BF16 = jnp.bfloat16

Q_ROWS = GROUP * BLOCK
LIST_AT = 2 * BLOCK
KV_ROWS = LIST_AT + 16
X_AT = 2 * Q_ROWS
QG_ROWS = X_AT + 48
COUNT_COL = TREE_B
OWN_COL = TREE_B + 1
VMEM_LIMIT = 14 << 20


def dot_nt(a, b):
    return lax.dot_general(a, b, (((1,), (1,)), ((), ())), preferred_element_type=F32)


def dot_nn(a, b):
    return lax.dot_general(a, b, (((1,), (0,)), ((), ())), preferred_element_type=F32)


def three_parts(array):
    high = array.astype(BF16)
    rest = array - high.astype(F32)
    middle = rest.astype(BF16)
    return high, middle, (rest - middle.astype(F32)).astype(BF16)


def in_vmem(count):
    return [pl.BlockSpec(memory_space=pltpu.VMEM)] * count


def call(kernel, name, in_specs, outs, scratch, micros, args, after=(), limit=VMEM_LIMIT):
    given = len(args)

    def body(*refs):
        kernel(*refs[:given], *refs[given + len(after) :])

    return pl.pallas_call(
        body,
        name=name,
        in_specs=[*in_specs, *[pl.BlockSpec(memory_space=pl.ANY)] * len(after)],
        out_specs=in_vmem(len(outs)),
        out_shape=[jax.ShapeDtypeStruct(*out) for out in outs],
        scratch_shapes=scratch,
        cost_estimate=pl.CostEstimate(flops=int(micros * 1e9), bytes_accessed=int(micros * 3e6), transcendentals=0),
        compiler_params=pltpu.CompilerParams(vmem_limit_bytes=limit),
    )(*args, *after)


def list_row(lists, rows):
    position, parity = lax.axis_index("blk"), lax.axis_index("head")
    me = lax.rem(position, KVH)
    first = (position - me) * 2
    rows[...] = jnp.full(rows.shape, -1.0, F32)
    rows[:2, :TREE_B] = lists[...].astype(F32)
    row = jnp.where(parity == 0, rows[0:1, :], rows[1:2, :])
    seen = row >= 0
    count = jnp.sum(jnp.where(seen, 1.0, 0.0)) - 1.0
    lane = lax.broadcasted_iota(jnp.int32, row.shape, 1)
    row = jnp.where(seen, row - first.astype(F32), -1.0)
    row = jnp.where(lane == COUNT_COL, count, row)
    row = jnp.where(lane == OWN_COL, (2 * me + parity).astype(F32), row)
    return me, jnp.broadcast_to(row, (KV_ROWS - LIST_AT, HD)).astype(BF16)


def kv_pack_kernel(key_in, value_in, lists_in, given, rows, key, value, lists, arrived):
    copies = [
        pltpu.make_async_copy(source, target, arrived.at[i])
        for i, (source, target) in enumerate(((lists_in, lists), (key_in, key), (value_in, value)))
    ]
    for copy in copies:
        copy.start()
    for copy in copies:
        copy.wait()
    me, tile = list_row(lists, rows)
    for i, chip in enumerate(CHIPS):
        columns = pl.ds(pl.multiple_of((me ^ (chip + 1)) * HD, HD), HD)
        given[i, :BLOCK, :] = key[:, columns]
        given[i, BLOCK:LIST_AT, :] = value[:, columns]
        given[i, LIST_AT:, :] = tile


def kv_pack(key_act, value_act, kv_lists):
    outs = [((len(CHIPS), KV_ROWS, HD), BF16)]
    args = (key_act, value_act, kv_lists)
    scratch = [pltpu.VMEM((8, HD), F32), *(pltpu.VMEM(arg.shape, arg.dtype) for arg in args), pltpu.SemaphoreType.DMA((3,))]
    specs = [pl.BlockSpec(memory_space=pl.ANY)] * 3
    return call(kv_pack_kernel, "kv_pack", specs, outs, scratch, 1, args, limit=60 << 20)[0]


def kv_pair_kernel(key, value, lists, theirs, *rest):
    pairs, rows = rest[:-1], rest[-1]
    me, tile = list_row(lists, rows)
    for i, (chip, pair) in enumerate(zip(CHIPS, pairs)):
        columns = pl.ds(pl.multiple_of((me ^ chip) * HD, HD), HD)
        pair[0, :BLOCK, :] = key[:, columns]
        pair[0, BLOCK:LIST_AT, :] = value[:, columns]
        pair[0, LIST_AT:, :] = tile
        pair[1] = theirs[i]


def kv_pair(key_act, value_act, kv_lists, theirs):
    outs = [((2, KV_ROWS, HD), BF16)] * len(CHIPS)
    args = (key_act, value_act, kv_lists, theirs)
    return call(kv_pair_kernel, "kv_pair", in_vmem(4), outs, [pltpu.VMEM((8, HD), F32)], 0.5, args)


def pair_up_kernel(mine, theirs, *pairs):
    for i, pair in enumerate(pairs):
        pair[0] = mine[i]
        pair[1] = theirs[i]


def pair_up(mine, theirs, after=()):
    outs = [((2, *mine.shape[1:]), mine.dtype)] * mine.shape[0]
    return call(pair_up_kernel, "pair_up", in_vmem(2), outs, [], 0.5, (mine, theirs), after)


def pass_on_kernel(source, target):
    target[...] = source[...]


def pass_on(array, after):
    return call(pass_on_kernel, "pass_on", in_vmem(1), [(array.shape, array.dtype)], [], 0.2, (array,), after)[0]


def kv_sum_kernel(mine, theirs, total):
    for i in range(mine.shape[0]):
        total[i] = (mine[i] + theirs[i].astype(F32)).astype(BF16)


def kv_sum(mine, theirs):
    return call(kv_sum_kernel, "kv_sum", in_vmem(2), [(mine.shape, BF16)], [], 0.5, (mine, theirs))[0]


def qg_pack_kernel(slots, query, grad, out, totals, *rest):
    packed, totals_by_group = rest[:-1], rest[-1]
    me = lax.rem(lax.axis_index("blk"), KVH)
    totals_by_group[...] = jnp.zeros(totals_by_group.shape, F32)
    for g in range(KVH):
        totals_by_group[g, :GROUP, :] = totals[g * GROUP : (g + 1) * GROUP, :]
    head_of = lax.broadcasted_iota(jnp.int32, (8, Q_ROWS), 1) // HD
    picks = jnp.where(head_of == lax.broadcasted_iota(jnp.int32, (8, Q_ROWS), 0), 1.0, 0.0).astype(BF16)
    for message, ks in zip(packed, slots):
        for n, k in enumerate(ks):
            columns = pl.ds(pl.multiple_of((me ^ k) * Q_ROWS, Q_ROWS), Q_ROWS)
            queries, grads = query[:, columns], grad[:, columns]
            for h in range(GROUP):
                message[n, h * BLOCK : (h + 1) * BLOCK, :] = queries[:, h * HD : (h + 1) * HD]
                message[n, Q_ROWS + h * BLOCK : Q_ROWS + (h + 1) * BLOCK, :] = grads[:, h * HD : (h + 1) * HD]
            product = grads.astype(F32) * out[:, columns].astype(F32)
            high = product.astype(BF16)
            low = (product - high.astype(F32)).astype(BF16)
            delta = dot_nt(picks, high) + dot_nt(picks, low)
            extras = jnp.concatenate([totals_by_group[me ^ k], delta], axis=0)
            for i, part in enumerate(three_parts(extras)):
                message[n, X_AT + 16 * i : X_AT + 16 * (i + 1), :] = part


def qg_pack(slots, query_act, grad_out, attn_out, totals, after):
    outs = [((len(ks), QG_ROWS, HD), BF16) for ks in slots]
    scratch = [pltpu.VMEM((KVH, 8, HD), F32)]
    args = (query_act, grad_out, attn_out, totals)
    return call(functools.partial(qg_pack_kernel, slots), "qg_pack", in_vmem(4), outs, scratch, 1, args, after)


def attend_kernel(ks, kind, *refs):
    refs = list(refs)
    opens, joins, closes = kind == "first", kind in ("join", "last"), kind == "last"
    lists = refs.pop(0)
    messages = []
    while len(messages) < len(ks):
        ref = refs.pop(0)
        messages += [ref.at[n] for n in range(ref.shape[0])]
    if opens:
        kv_own, kv_other = [refs.pop(0) for _ in CHIPS], [refs.pop(0) for _ in CHIPS]
    else:
        keys, keys_t, values, sums_in = (refs.pop(0) for _ in range(4))
    if joins:
        earlier = refs.pop(0)
        backs = [refs.pop(0) for _ in ks]
        for n, back in enumerate(backs):
            back[0] = earlier[n]
        query_grads = [back.at[1] for back in backs]
    else:
        back = refs.pop(0)
        query_grads = [back.at[n] for n in range(len(ks))]
    if closes:
        mine, others = [refs.pop(0) for _ in BACK_HALVES], [refs.pop(0) for _ in BACK_HALVES]
    if opens:
        keys, keys_t, values = (refs.pop(0) for _ in range(3))
    sums = refs.pop(0)
    query_sum, probs_held, scores_held = refs
    me, parity = lists[0, OWN_COL] // 2, lists[0, OWN_COL] % 2
    spare = 2 * KVH

    if opens:
        for own, other, chip in zip(kv_own, kv_other, CHIPS):
            for n in range(2):
                at = 2 * (me ^ (chip + n))
                for ref, j in ((own, at + parity), (other, at + 1 - parity)):
                    keys[j] = ref[n, :BLOCK, :]
                    values[j] = ref[n, BLOCK:LIST_AT, :]
                    keys_t[j] = ref[n, :BLOCK, :].T
        zero = jnp.zeros((BLOCK, HD), BF16)
        keys[spare], keys_t[spare], values[spare] = zero, zero, zero
        sums[...] = jnp.zeros(sums.shape, F32)
    else:
        sums[...] = sums_in[...]

    def both(ref, pair, axis):
        return jnp.concatenate([ref[j] for j in pair], axis=axis)

    def produce(n, pair, extras, diagonal):
        totals, deltas = extras
        scores = dot_nt(both(keys, pair, 0), messages[n][:Q_ROWS, :])
        probs = jnp.exp2(scores * (SCALING * math.log2(math.e)) - totals)
        if diagonal:
            at_key = lax.broadcasted_iota(jnp.int32, probs.shape, 0) - BLOCK
            at_query = lax.broadcasted_iota(jnp.int32, probs.shape, 1) % BLOCK
            probs = jnp.where(at_key <= at_query, probs, 0.0)
        grad_probs = dot_nt(both(values, pair, 0), messages[n][Q_ROWS:X_AT, :])
        probs_held[...] = probs.astype(BF16)
        scores_held[...] = (probs * (grad_probs - deltas)).astype(BF16)

    def consume(n, pair):
        probs_low, grad_scores = probs_held[...], scores_held[...]
        value_part = dot_nn(probs_low, messages[n][Q_ROWS:X_AT, :])
        key_part = dot_nn(grad_scores, messages[n][:Q_ROWS, :])
        query_sum[...] += dot_nn(both(keys_t, pair, 1), grad_scores)
        for i, j in enumerate(pair):
            sums[j, :BLOCK, :] += key_part[i * BLOCK : (i + 1) * BLOCK, :]
            sums[j, BLOCK:, :] += value_part[i * BLOCK : (i + 1) * BLOCK, :]

    def finish(n):
        for h in range(GROUP):
            part = query_sum[:, h * BLOCK : (h + 1) * BLOCK].T
            query_grads[n][h * BLOCK : (h + 1) * BLOCK, :] = (part * SCALING).astype(BF16)

    pair = None
    for n, k in enumerate(ks):
        parts = [messages[n][X_AT + 16 * i : X_AT + 16 * (i + 1), :].astype(F32) for i in range(3)]
        rows = parts[0] + parts[1] + parts[2]
        totals = jnp.concatenate([rows[h : h + 1, :] for h in range(GROUP)], axis=1) * math.log2(math.e)
        deltas = jnp.concatenate([rows[8 + h : 9 + h, :] for h in range(GROUP)], axis=1)
        extras = (totals, deltas)
        count = lists[k, COUNT_COL]
        pairs = count // 2
        left = jnp.where(count % 2 == 1, lists[k, jnp.maximum(count - 1, 0)], spare)
        if pair is not None:
            consume(n - 1, pair)
        produce(n, (left, lists[k, OWN_COL]), extras, True)
        if pair is not None:
            finish(n - 1)
        query_sum[...] = jnp.zeros(query_sum.shape, F32)

        def visit(t, held):
            consume(n, held)
            following = (lists[k, 2 * t], lists[k, 2 * t + 1])
            produce(n, following, extras, False)
            return following

        pair = lax.fori_loop(0, pairs, visit, (left, lists[k, OWN_COL]))
    consume(len(ks) - 1, pair)
    finish(len(ks) - 1)

    if closes:
        for half, own, other in zip(BACK_HALVES, mine, others):
            for i, k in enumerate(half):
                at = 2 * (me ^ k)
                own[i, :BLOCK, :] = sums[at + parity, :BLOCK, :] * SCALING
                own[i, BLOCK:, :] = sums[at + parity, BLOCK:, :]
                other[i, :BLOCK, :] = (sums[at + 1 - parity, :BLOCK, :] * SCALING).astype(BF16)
                other[i, BLOCK:, :] = sums[at + 1 - parity, BLOCK:, :].astype(BF16)


def attend(name, kind, ks, lists, messages, state, micros):
    blocks = 2 * KVH + 1
    sums = ((blocks, 2 * BLOCK, HD), F32)
    scratch = []
    if kind in ("join", "last"):
        outs = [((2, Q_ROWS, HD), BF16)] * len(ks)
    else:
        outs = [((len(ks), Q_ROWS, HD), BF16)]
    if kind == "first":
        outs += [((blocks, BLOCK, HD), BF16)] * 3
    if kind == "last":
        outs += [((KVH // 2, 2 * BLOCK, HD), kind) for kind in (F32, F32, BF16, BF16)]
        scratch = [pltpu.VMEM(*sums)]
    else:
        outs += [sums]
    scratch += [pltpu.VMEM((HD, Q_ROWS), F32), pltpu.VMEM((2 * BLOCK, Q_ROWS), BF16), pltpu.VMEM((2 * BLOCK, Q_ROWS), BF16)]
    specs = [pl.BlockSpec(memory_space=pltpu.SMEM)] + in_vmem(len(messages) + len(state))
    kernel = functools.partial(attend_kernel, ks, kind)
    return call(kernel, name, specs, outs, scratch, micros, (lists, *messages, *state))


def query_relay_kernel(own, *refs):
    given = refs[-1]
    given[0] = own[1]
    for i, back in enumerate(refs[:-1]):
        given[i + 1] = back[1]


def query_unpack_kernel(*refs):
    backs, theirs, query_grad, done = refs[: len(CHIPS)], *refs[len(CHIPS) :]
    done[...] = jnp.zeros(done.shape, F32)
    me = lax.rem(lax.axis_index("blk"), KVH)
    for i, chip in enumerate(CHIPS):
        for k, ref, n in ((chip, backs[i], 0), (chip + 1, theirs, i)):
            for h in range(GROUP):
                columns = pl.ds(pl.multiple_of(((me ^ k) * GROUP + h) * HD, HD), HD)
                query_grad[:, columns] = ref[n, h * BLOCK : (h + 1) * BLOCK, :]


def kv_unpack_kernel(*refs):
    key_grad, value_grad = refs[len(CHIPS) :]
    me = lax.rem(lax.axis_index("blk"), KVH)
    for chip, pair in zip(reversed(CHIPS), refs):
        for n in range(2):
            columns = pl.ds(pl.multiple_of((me ^ (chip + n)) * HD, HD), HD)
            key_grad[:, columns] = pair[n, :BLOCK, :]
            value_grad[:, columns] = pair[n, BLOCK:, :]


CHIPS = (0, 2, 4, 6)
CHIPS = (0, 2, 4, 6)
VISITS = (("first", (0, 1)), ("more", (6, 7)), ("more", (2, 4)), ("last", (3, 5)))
EXPECTED = (0.5, 0.5, 0.5, 6)
BACK_HALVES = ((1, 3, 5, 7), CHIPS)


def by_trees(query_act, key_act, value_act, attn_out, grad_out, log_sum, kv_lists):
    size = lax.axis_size("blk")

    def exchanged(array, k):
        return lax.ppermute(array, "blk", [(i, i ^ k) for i in range(size)])

    def swapped(array):
        return lax.ppermute(array, "head", [(0, 1), (1, 0)])

    def by_chip(pairs):
        moved = {chip: exchanged(pair, chip) for chip, pair in reversed(list(zip(CHIPS, pairs))) if chip}
        return [moved.get(chip, pair) for chip, pair in zip(CHIPS, pairs)]

    given = kv_pack(key_act, value_act, kv_lists)
    paired = kv_pair(key_act, value_act, kv_lists, exchanged(given, 1))
    kv_own = by_chip(paired)
    kv_other = [swapped(part) for part in kv_own]
    lists = jnp.concatenate([part[:, LIST_AT, : OWN_COL + 1] for part in kv_own]).astype(jnp.int32)

    qg = (query_act, grad_out, attn_out, log_sum.T)
    beside = exchanged(qg_pack(((1, 7),), *qg, (paired[1],))[0], 1)
    own, far = qg_pack(((0,), (6,)), *qg, (kv_other[0],))
    far = pair_up(far, beside[1:], (*kv_own[:0:-1], kv_other[0]))[0]
    here = [[own, beside[:1]], [exchanged(far, 6)]]
    for ks, after in (((2, 4), kv_other[2]), ((3, 5), kv_other[3])):
        sent = qg_pack([(k,) for k in ks], *qg, (after,))
        here.append([exchanged(message, k) for k, message in zip(ks, sent)])

    state, grads = (*kv_own, *kv_other), []
    for i, (kind, ks) in enumerate(VISITS):
        if kind == "last":
            state = (*state, grads[-1])
        results = attend(f"attend_{i}", kind, ks, lists, here[i], state, EXPECTED[i])
        grads.append(results[0])
        state = tuple(results[1:]) if kind == "first" else (*state[:3], results[-1])
    far_back = exchanged(grads[1], 6)
    backs = [exchanged(results[0], 2), exchanged(results[1], 4), far_back]
    others = (pass_on(results[4], (far_back,)), results[5])
    theirs = [swapped(other) for other in others]
    given, kept = [kv_sum(mine, other) for mine, other in zip(results[2:4], theirs)]
    paired = pair_up(kept, exchanged(given, 1))
    kv_back = by_chip(paired)
    outs = [((4, Q_ROWS, HD), BF16)]
    given = call(query_relay_kernel, "query_relay", in_vmem(4), outs, [], 0.5, (grads[0], *backs), paired[:1])[0]
    args = (grads[0], *backs, exchanged(given, 1))
    outs = [((BLOCK, QH * HD), BF16), ((8, HD), F32)]
    grad_query, done = call(query_unpack_kernel, "query_unpack", in_vmem(5), outs, [], 1, args)
    outs = [((BLOCK, KVH * HD), BF16)] * 2
    grad_key, grad_value = call(kv_unpack_kernel, "kv_unpack", in_vmem(4), outs, [], 1, kv_back[::-1], (done,))
    return grad_query, grad_key, grad_value


def passed_along(array, axis, by):
    size = lax.axis_size(axis)
    pairs = [(i, i + by) for i in range(size) if 0 <= i + by < size]
    return lax.ppermute(array, axis, pairs)


def shifted(array, axis, by):
    size = lax.axis_size(axis)
    return lax.ppermute(array, axis, [(i, (i + by) % size) for i in range(size)])


def head_delta(grad_rows, out_rows, heads):
    count = grad_rows.shape[0]
    return jnp.einsum(
        "thd,thd->th",
        grad_rows.reshape(count, heads, HD),
        out_rows.reshape(count, heads, HD),
        preferred_element_type=jnp.float32,
    )


def by_ring(query_act, key_act, value_act, attn_out, grad_out, log_sum, kv_lists):
    head_count = lax.axis_size("head")
    blk_count = lax.axis_size("blk")
    sent_delta = head_delta(grad_out, attn_out, QH)
    query_rows, key_rows, value_rows, grad_rows, total_rows, delta_rows = (
        lax.all_to_all(
            query_act.astype(jnp.float32), "head", split_axis=1, concat_axis=0, tiled=True
        ).astype(query_act.dtype),
        lax.all_to_all(
            key_act.astype(jnp.float32), "head", split_axis=1, concat_axis=0, tiled=True
        ).astype(key_act.dtype),
        lax.all_to_all(
            value_act.astype(jnp.float32), "head", split_axis=1, concat_axis=0, tiled=True
        ).astype(value_act.dtype),
        lax.all_to_all(
            grad_out.astype(jnp.float32), "head", split_axis=1, concat_axis=0, tiled=True
        ).astype(grad_out.dtype),
        lax.all_to_all(log_sum, "head", split_axis=1, concat_axis=0, tiled=True),
        lax.all_to_all(sent_delta, "head", split_axis=1, concat_axis=0, tiled=True),
    )
    tokens = query_rows.shape[0]
    local_heads = KVH // head_count
    group_size = QH // KVH
    blocks_dev = tokens // BLOCK
    scaling = HD ** (-0.5)
    queries = query_rows.reshape(tokens, local_heads, group_size, HD)
    out_grads = grad_rows.reshape(tokens, local_heads, group_size, HD)
    row_totals = total_rows.reshape(tokens, local_heads, group_size).transpose(1, 2, 0)[
        :, :, :, None
    ]
    row_deltas = delta_rows.reshape(tokens, local_heads, group_size).transpose(1, 2, 0)[
        :, :, :, None
    ]
    position = lax.axis_index("blk")
    query_pos = position * tokens + jnp.arange(tokens, dtype=jnp.int32)

    def block_mask(rotation):
        source = (position - rotation) % blk_count
        key_ids = source * blocks_dev + jnp.arange(blocks_dev, dtype=jnp.int32)
        listed = jnp.any(kv_lists[:, :, None] == key_ids[None, None, :], axis=1)
        key_pos = source * tokens + jnp.arange(tokens, dtype=jnp.int32)
        return (listed, key_pos)

    def attend(kv_pair, key_sums, query_grad, listed, key_pos):
        visible = jnp.repeat(jnp.repeat(listed, BLOCK, axis=0), BLOCK, axis=1) & (
            key_pos[None, :] <= query_pos[:, None]
        )
        key_block = kv_pair[0].reshape(tokens, local_heads, HD)
        value_block = kv_pair[1].reshape(tokens, local_heads, HD)
        scores = (
            jnp.einsum("tkgd,skd->kgts", queries, key_block, preferred_element_type=jnp.float32)
            * scaling
        )
        weights = jnp.where(visible, jnp.exp(scores - row_totals), 0.0)
        grad_probs = jnp.einsum(
            "tkgd,skd->kgts", out_grads, value_block, preferred_element_type=jnp.float32
        )
        grad_scores = (weights * (grad_probs - row_deltas)).astype(jnp.bfloat16)
        probs_low = weights.astype(jnp.bfloat16)
        value_part = jnp.einsum(
            "kgts,tkgd->skd", probs_low, out_grads, preferred_element_type=jnp.float32
        )
        key_part = (
            jnp.einsum("kgts,tkgd->skd", grad_scores, queries, preferred_element_type=jnp.float32)
            * scaling
        )
        query_part = (
            jnp.einsum("kgts,skd->tkgd", grad_scores, key_block, preferred_element_type=jnp.float32)
            * scaling
        )
        added = jnp.stack(
            [
                key_part.reshape(tokens, local_heads * HD),
                value_part.reshape(tokens, local_heads * HD),
            ]
        )
        return (key_sums + added, query_grad + query_part)

    def visit(rotation, kv_pair, key_sums, query_grad):
        listed, key_pos = block_mask(rotation)
        return attend(kv_pair, key_sums, query_grad, listed, key_pos)

    kv_pair = jnp.stack([key_rows, value_rows])
    empty_sums = jnp.zeros((2, tokens, local_heads * HD), jnp.float32)
    empty_grad = jnp.zeros((tokens, local_heads, group_size, HD), jnp.float32)

    def advance(rotation, carried):
        kv_here, key_sums, query_grad = carried
        arrived = passed_along(kv_here, "blk", 1)
        key_sums, query_grad = visit(rotation, kv_here, key_sums, query_grad)
        key_sums = shifted(key_sums, "blk", 1)
        return (arrived, key_sums, query_grad)

    kv_here, key_sums, query_grad = lax.fori_loop(
        0, blk_count - 1, advance, (kv_pair, empty_sums, empty_grad)
    )
    key_sums, query_grad = visit(blk_count - 1, kv_here, key_sums, query_grad)
    key_sums = shifted(key_sums.astype(jnp.bfloat16), "blk", 1 - blk_count).astype(key_sums.dtype)
    query_low = query_grad.reshape(tokens, local_heads * group_size * HD).astype(jnp.bfloat16)
    key_low = key_sums[0].astype(jnp.bfloat16)
    value_low = key_sums[1].astype(jnp.bfloat16)
    grad_query, grad_key, grad_value = (
        lax.all_to_all(query_low, "head", split_axis=0, concat_axis=1, tiled=True),
        lax.all_to_all(key_low, "head", split_axis=0, concat_axis=1, tiled=True),
        lax.all_to_all(value_low, "head", split_axis=0, concat_axis=1, tiled=True),
    )
    return (grad_query, grad_key, grad_value)


def local(query_act, *others):
    head_count = lax.axis_size("head")
    blk_count = lax.axis_size("blk")
    if query_act.shape[0] == BLOCK and head_count == 2 and blk_count == 2 * KVH and blk_count * head_count == TREE_B:
        return by_trees(query_act, *others)
    return by_ring(query_act, *others)


def solution(mesh):
    rows = P(("blk", "head"), None)
    return jax.shard_map(
        local,
        mesh=mesh,
        in_specs=(rows,) * 6 + (P("blk", None),),
        out_specs=(rows,) * 3,
        check_vma=False,
    )
```

```python
import functools
import math

import jax
import jax.numpy as jnp
from jax import lax
from jax.experimental import pallas as pl
from jax.experimental.pallas import tpu as pltpu
from jax.sharding import PartitionSpec as P

QH = 40
KVH = 8
HD = 128
BLOCK = 128
TREE_B = 32
GROUP = QH // KVH
SCALING = HD ** (-0.5)
F32 = jnp.float32
BF16 = jnp.bfloat16

Q_ROWS = GROUP * BLOCK
LIST_AT = 2 * BLOCK
KV_ROWS = LIST_AT + 16
X_AT = 2 * Q_ROWS
QG_ROWS = X_AT + 48
COUNT_COL = TREE_B
OWN_COL = TREE_B + 1
VMEM_LIMIT = 14 << 20


def dot_nt(a, b):
    return lax.dot_general(a, b, (((1,), (1,)), ((), ())), preferred_element_type=F32)


def dot_nn(a, b):
    return lax.dot_general(a, b, (((1,), (0,)), ((), ())), preferred_element_type=F32)


def three_parts(array):
    high = array.astype(BF16)
    rest = array - high.astype(F32)
    middle = rest.astype(BF16)
    return high, middle, (rest - middle.astype(F32)).astype(BF16)


def in_vmem(count):
    return [pl.BlockSpec(memory_space=pltpu.VMEM)] * count


def call(kernel, name, in_specs, outs, scratch, micros, args, after=(), limit=VMEM_LIMIT):
    given = len(args)

    def body(*refs):
        kernel(*refs[:given], *refs[given + len(after) :])

    return pl.pallas_call(
        body,
        name=name,
        in_specs=[*in_specs, *[pl.BlockSpec(memory_space=pl.ANY)] * len(after)],
        out_specs=in_vmem(len(outs)),
        out_shape=[jax.ShapeDtypeStruct(*out) for out in outs],
        scratch_shapes=scratch,
        cost_estimate=pl.CostEstimate(flops=int(micros * 1e9), bytes_accessed=int(micros * 3e6), transcendentals=0),
        compiler_params=pltpu.CompilerParams(vmem_limit_bytes=limit),
    )(*args, *after)


def list_row(lists, rows):
    position, parity = lax.axis_index("blk"), lax.axis_index("head")
    me = lax.rem(position, KVH)
    first = (position - me) * 2
    rows[...] = jnp.full(rows.shape, -1.0, F32)
    rows[:2, :TREE_B] = lists[...].astype(F32)
    row = jnp.where(parity == 0, rows[0:1, :], rows[1:2, :])
    seen = row >= 0
    count = jnp.sum(jnp.where(seen, 1.0, 0.0)) - 1.0
    lane = lax.broadcasted_iota(jnp.int32, row.shape, 1)
    row = jnp.where(seen, row - first.astype(F32), -1.0)
    row = jnp.where(lane == COUNT_COL, count, row)
    row = jnp.where(lane == OWN_COL, (2 * me + parity).astype(F32), row)
    return me, jnp.broadcast_to(row, (KV_ROWS - LIST_AT, HD)).astype(BF16)


def kv_pack_kernel(key_in, value_in, lists_in, given, rows, key, value, lists, arrived):
    copies = [
        pltpu.make_async_copy(source, target, arrived.at[i])
        for i, (source, target) in enumerate(((lists_in, lists), (key_in, key), (value_in, value)))
    ]
    for copy in copies:
        copy.start()
    for copy in copies:
        copy.wait()
    me, tile = list_row(lists, rows)
    for i, chip in enumerate(CHIPS):
        columns = pl.ds(pl.multiple_of((me ^ (chip + 1)) * HD, HD), HD)
        given[i, :BLOCK, :] = key[:, columns]
        given[i, BLOCK:LIST_AT, :] = value[:, columns]
        given[i, LIST_AT:, :] = tile


def kv_pack(key_act, value_act, kv_lists):
    outs = [((len(CHIPS), KV_ROWS, HD), BF16)]
    args = (key_act, value_act, kv_lists)
    scratch = [pltpu.VMEM((8, HD), F32), *(pltpu.VMEM(arg.shape, arg.dtype) for arg in args), pltpu.SemaphoreType.DMA((3,))]
    specs = [pl.BlockSpec(memory_space=pl.ANY)] * 3
    return call(kv_pack_kernel, "kv_pack", specs, outs, scratch, 1, args, limit=60 << 20)[0]


def kv_pair_kernel(key, value, lists, theirs, *rest):
    pairs, rows = rest[:-1], rest[-1]
    me, tile = list_row(lists, rows)
    for i, (chip, pair) in enumerate(zip(CHIPS, pairs)):
        columns = pl.ds(pl.multiple_of((me ^ chip) * HD, HD), HD)
        pair[0, :BLOCK, :] = key[:, columns]
        pair[0, BLOCK:LIST_AT, :] = value[:, columns]
        pair[0, LIST_AT:, :] = tile
        pair[1] = theirs[i]


def kv_pair(key_act, value_act, kv_lists, theirs):
    outs = [((2, KV_ROWS, HD), BF16)] * len(CHIPS)
    args = (key_act, value_act, kv_lists, theirs)
    return call(kv_pair_kernel, "kv_pair", in_vmem(4), outs, [pltpu.VMEM((8, HD), F32)], 0.5, args)


def pair_up_kernel(mine, theirs, *pairs):
    for i, pair in enumerate(pairs):
        pair[0] = mine[i]
        pair[1] = theirs[i]


def pair_up(mine, theirs, after=()):
    outs = [((2, *mine.shape[1:]), mine.dtype)] * mine.shape[0]
    return call(pair_up_kernel, "pair_up", in_vmem(2), outs, [], 0.5, (mine, theirs), after)


def pass_on_kernel(source, target):
    target[...] = source[...]


def pass_on(array, after):
    return call(pass_on_kernel, "pass_on", in_vmem(1), [(array.shape, array.dtype)], [], 0.2, (array,), after)[0]


def kv_sum_kernel(mine, theirs, total):
    for i in range(mine.shape[0]):
        total[i] = (mine[i] + theirs[i].astype(F32)).astype(BF16)


def kv_sum(mine, theirs):
    return call(kv_sum_kernel, "kv_sum", in_vmem(2), [(mine.shape, BF16)], [], 0.5, (mine, theirs))[0]


def qg_pack_kernel(slots, query, grad, out, totals, *rest):
    packed, totals_by_group = rest[:-1], rest[-1]
    me = lax.rem(lax.axis_index("blk"), KVH)
    totals_by_group[...] = jnp.zeros(totals_by_group.shape, F32)
    for g in range(KVH):
        totals_by_group[g, :GROUP, :] = totals[g * GROUP : (g + 1) * GROUP, :]
    head_of = lax.broadcasted_iota(jnp.int32, (8, Q_ROWS), 1) // HD
    picks = jnp.where(head_of == lax.broadcasted_iota(jnp.int32, (8, Q_ROWS), 0), 1.0, 0.0).astype(BF16)
    for message, ks in zip(packed, slots):
        for n, k in enumerate(ks):
            columns = pl.ds(pl.multiple_of((me ^ k) * Q_ROWS, Q_ROWS), Q_ROWS)
            queries, grads = query[:, columns], grad[:, columns]
            for h in range(GROUP):
                message[n, h * BLOCK : (h + 1) * BLOCK, :] = queries[:, h * HD : (h + 1) * HD]
                message[n, Q_ROWS + h * BLOCK : Q_ROWS + (h + 1) * BLOCK, :] = grads[:, h * HD : (h + 1) * HD]
            product = grads.astype(F32) * out[:, columns].astype(F32)
            high = product.astype(BF16)
            low = (product - high.astype(F32)).astype(BF16)
            delta = dot_nt(picks, high) + dot_nt(picks, low)
            extras = jnp.concatenate([totals_by_group[me ^ k], delta], axis=0)
            for i, part in enumerate(three_parts(extras)):
                message[n, X_AT + 16 * i : X_AT + 16 * (i + 1), :] = part


def qg_pack(slots, query_act, grad_out, attn_out, totals, after):
    outs = [((len(ks), QG_ROWS, HD), BF16) for ks in slots]
    scratch = [pltpu.VMEM((KVH, 8, HD), F32)]
    args = (query_act, grad_out, attn_out, totals)
    return call(functools.partial(qg_pack_kernel, slots), "qg_pack", in_vmem(4), outs, scratch, 1, args, after)


def attend_kernel(ks, kind, width, *refs):
    refs = list(refs)
    opens, joins, closes = kind == "first", kind in ("join", "last"), kind == "last"
    lists = refs.pop(0)
    messages = []
    while len(messages) < len(ks):
        ref = refs.pop(0)
        messages += [ref.at[n] for n in range(ref.shape[0])]
    if opens:
        kv_own, kv_other = [refs.pop(0) for _ in CHIPS], [refs.pop(0) for _ in CHIPS]
    else:
        keys, keys_t, values, sums_in = (refs.pop(0) for _ in range(4))
    if joins:
        earlier = refs.pop(0)
        backs = [refs.pop(0) for _ in ks]
        for n, back in enumerate(backs):
            back[0] = earlier[n]
        query_grads = [back.at[1] for back in backs]
    else:
        back = refs.pop(0)
        query_grads = [back.at[n] for n in range(len(ks))]
    if closes:
        mine, others = [refs.pop(0) for _ in BACK_HALVES], [refs.pop(0) for _ in BACK_HALVES]
    if opens:
        keys, keys_t, values = (refs.pop(0) for _ in range(3))
    sums = refs.pop(0)
    query_sum, probs_held, scores_held = refs
    me, parity = lists[0, OWN_COL] // 2, lists[0, OWN_COL] % 2
    spare = 2 * KVH

    if opens:
        for own, other, chip in zip(kv_own, kv_other, CHIPS):
            for n in range(2):
                at = 2 * (me ^ (chip + n))
                for ref, j in ((own, at + parity), (other, at + 1 - parity)):
                    keys[j] = ref[n, :BLOCK, :]
                    values[j] = ref[n, BLOCK:LIST_AT, :]
                    keys_t[j] = ref[n, :BLOCK, :].T
        zero = jnp.zeros((BLOCK, HD), BF16)
        keys[spare], keys_t[spare], values[spare] = zero, zero, zero
        sums[...] = jnp.zeros(sums.shape, F32)
    else:
        sums[...] = sums_in[...]

    def both(ref, pair, axis):
        return jnp.concatenate([ref[j] for j in pair], axis=axis)

    def produce(n, pair, extras, diagonal):
        totals, deltas = extras
        scores = dot_nt(both(keys, pair, 0), messages[n][:Q_ROWS, :])
        probs = jnp.exp2(scores * (SCALING * math.log2(math.e)) - totals)
        if diagonal:
            at_key = lax.broadcasted_iota(jnp.int32, probs.shape, 0) - (width - 1) * BLOCK
            at_query = lax.broadcasted_iota(jnp.int32, probs.shape, 1) % BLOCK
            probs = jnp.where(at_key <= at_query, probs, 0.0)
        grad_probs = dot_nt(both(values, pair, 0), messages[n][Q_ROWS:X_AT, :])
        probs_held[...] = probs.astype(BF16)
        scores_held[...] = (probs * (grad_probs - deltas)).astype(BF16)

    def consume(n, pair):
        probs_low, grad_scores = probs_held[...], scores_held[...]
        value_part = dot_nn(probs_low, messages[n][Q_ROWS:X_AT, :])
        key_part = dot_nn(grad_scores, messages[n][:Q_ROWS, :])
        query_sum[...] += dot_nn(both(keys_t, pair, 1), grad_scores)
        for i, j in enumerate(pair):
            sums[j, :BLOCK, :] += key_part[i * BLOCK : (i + 1) * BLOCK, :]
            sums[j, BLOCK:, :] += value_part[i * BLOCK : (i + 1) * BLOCK, :]

    def finish(n):
        for h in range(GROUP):
            part = query_sum[:, h * BLOCK : (h + 1) * BLOCK].T
            query_grads[n][h * BLOCK : (h + 1) * BLOCK, :] = (part * SCALING).astype(BF16)

    pair = None
    for n, k in enumerate(ks):
        parts = [messages[n][X_AT + 16 * i : X_AT + 16 * (i + 1), :].astype(F32) for i in range(3)]
        rows = parts[0] + parts[1] + parts[2]
        totals = jnp.concatenate([rows[h : h + 1, :] for h in range(GROUP)], axis=1) * math.log2(math.e)
        deltas = jnp.concatenate([rows[8 + h : 9 + h, :] for h in range(GROUP)], axis=1)
        extras = (totals, deltas)
        count = lists[k, COUNT_COL]
        steps = count // width
        left = count - steps * width
        first = tuple(
            jnp.where(i < left, lists[k, jnp.minimum(steps * width + i, TREE_B - 1)], spare) for i in range(width - 1)
        ) + (lists[k, OWN_COL],)
        if pair is not None:
            consume(n - 1, pair)
        produce(n, first, extras, True)
        if pair is not None:
            finish(n - 1)
        query_sum[...] = jnp.zeros(query_sum.shape, F32)

        def visit(t, held):
            consume(n, held)
            following = tuple(lists[k, width * t + i] for i in range(width))
            produce(n, following, extras, False)
            return following

        pair = lax.fori_loop(0, steps, visit, first)
    consume(len(ks) - 1, pair)
    finish(len(ks) - 1)

    if closes:
        for half, own, other in zip(BACK_HALVES, mine, others):
            for i, k in enumerate(half):
                at = 2 * (me ^ k)
                own[i, :BLOCK, :] = sums[at + parity, :BLOCK, :] * SCALING
                own[i, BLOCK:, :] = sums[at + parity, BLOCK:, :]
                other[i, :BLOCK, :] = (sums[at + 1 - parity, :BLOCK, :] * SCALING).astype(BF16)
                other[i, BLOCK:, :] = sums[at + 1 - parity, BLOCK:, :].astype(BF16)


def attend(name, kind, ks, width, lists, messages, state, micros):
    blocks = 2 * KVH + 1
    sums = ((blocks, 2 * BLOCK, HD), F32)
    scratch = []
    if kind in ("join", "last"):
        outs = [((2, Q_ROWS, HD), BF16)] * len(ks)
    else:
        outs = [((len(ks), Q_ROWS, HD), BF16)]
    if kind == "first":
        outs += [((blocks, BLOCK, HD), BF16)] * 3
    if kind == "last":
        outs += [((KVH // 2, 2 * BLOCK, HD), kind) for kind in (F32, F32, BF16, BF16)]
        scratch = [pltpu.VMEM(*sums)]
    else:
        outs += [sums]
    scratch += [pltpu.VMEM((HD, Q_ROWS), F32), pltpu.VMEM((width * BLOCK, Q_ROWS), BF16), pltpu.VMEM((width * BLOCK, Q_ROWS), BF16)]
    specs = [pl.BlockSpec(memory_space=pltpu.SMEM)] + in_vmem(len(messages) + len(state))
    kernel = functools.partial(attend_kernel, ks, kind, width)
    return call(kernel, name, specs, outs, scratch, micros, (lists, *messages, *state))


def query_relay_kernel(own, *refs):
    given = refs[-1]
    given[0] = own[1]
    for i, back in enumerate(refs[:-1]):
        given[i + 1] = back[1]


def query_unpack_kernel(*refs):
    backs, theirs, query_grad, done = refs[: len(CHIPS)], *refs[len(CHIPS) :]
    done[...] = jnp.zeros(done.shape, F32)
    me = lax.rem(lax.axis_index("blk"), KVH)
    for i, chip in enumerate(CHIPS):
        for k, ref, n in ((chip, backs[i], 0), (chip + 1, theirs, i)):
            for h in range(GROUP):
                columns = pl.ds(pl.multiple_of(((me ^ k) * GROUP + h) * HD, HD), HD)
                query_grad[:, columns] = ref[n, h * BLOCK : (h + 1) * BLOCK, :]


def kv_unpack_kernel(*refs):
    key_grad, value_grad = refs[len(CHIPS) :]
    me = lax.rem(lax.axis_index("blk"), KVH)
    for i, chip in enumerate(CHIPS):
        for n in range(2):
            columns = pl.ds(pl.multiple_of((me ^ (chip + n)) * HD, HD), HD)
            key_grad[:, columns] = refs[i][n, :BLOCK, :]
            value_grad[:, columns] = refs[i][n, BLOCK:, :]


CHIPS = (0, 2, 4, 6)
CHIPS = (0, 2, 4, 6)
VISITS = (("first", (0, 1)), ("more", (6, 7)), ("more", (2, 4)), ("last", (3, 5)))
EXPECTED = (0.5, 0.5, 0.5, 6)
WIDTHS = (2, 4, 2, 4)
BACK_HALVES = ((1, 3, 5, 7), CHIPS)


def by_trees(query_act, key_act, value_act, attn_out, grad_out, log_sum, kv_lists):
    size = lax.axis_size("blk")

    def exchanged(array, k):
        return lax.ppermute(array, "blk", [(i, i ^ k) for i in range(size)])

    def swapped(array):
        return lax.ppermute(array, "head", [(0, 1), (1, 0)])

    given = kv_pack(key_act, value_act, kv_lists)
    paired = kv_pair(key_act, value_act, kv_lists, exchanged(given, 1))
    kv_own = [paired[0], *(exchanged(part, chip) for part, chip in zip(paired[1:], CHIPS[1:]))]
    kv_other = [swapped(part) for part in kv_own]
    lists = jnp.concatenate([part[:, LIST_AT, : OWN_COL + 1] for part in kv_own]).astype(jnp.int32)

    qg = (query_act, grad_out, attn_out, log_sum.T)
    beside = exchanged(qg_pack(((1, 7),), *qg, (paired[1],))[0], 1)
    own, far = qg_pack(((0,), (6,)), *qg, (kv_other[0],))
    far = pair_up(far, beside[1:], (*kv_own[1:], kv_other[0]))[0]
    here = [[own, beside[:1]], [exchanged(far, 6)]]
    for ks, after in (((2, 4), kv_other[2]), ((3, 5), kv_other[3])):
        sent = qg_pack([(k,) for k in ks], *qg, (after,))
        here.append([exchanged(message, k) for k, message in zip(ks, sent)])

    state, grads = (*kv_own, *kv_other), []
    for i, (kind, ks) in enumerate(VISITS):
        if kind == "last":
            state = (*state, grads[-1])
        results = attend(f"attend_{i}", kind, ks, WIDTHS[i], lists, here[i], state, EXPECTED[i])
        grads.append(results[0])
        state = tuple(results[1:]) if kind == "first" else (*state[:3], results[-1])
    far_back = exchanged(grads[1], 6)
    backs = [exchanged(results[0], 2), exchanged(results[1], 4), far_back]
    others = (pass_on(results[4], (far_back,)), results[5])
    theirs = [swapped(other) for other in others]
    given, kept = [kv_sum(mine, other) for mine, other in zip(results[2:4], theirs)]
    paired = pair_up(kept, exchanged(given, 1))
    kv_back = [paired[0], *(exchanged(pair, chip) for pair, chip in zip(paired[1:], CHIPS[1:]))]
    outs = [((4, Q_ROWS, HD), BF16)]
    given = call(query_relay_kernel, "query_relay", in_vmem(4), outs, [], 0.5, (grads[0], *backs), paired[:1])[0]
    args = (grads[0], *backs, exchanged(given, 1))
    outs = [((BLOCK, QH * HD), BF16), ((8, HD), F32)]
    grad_query, done = call(query_unpack_kernel, "query_unpack", in_vmem(5), outs, [], 1, args)
    outs = [((BLOCK, KVH * HD), BF16)] * 2
    grad_key, grad_value = call(kv_unpack_kernel, "kv_unpack", in_vmem(4), outs, [], 1, kv_back, (done,))
    return grad_query, grad_key, grad_value


def passed_along(array, axis, by):
    size = lax.axis_size(axis)
    pairs = [(i, i + by) for i in range(size) if 0 <= i + by < size]
    return lax.ppermute(array, axis, pairs)


def shifted(array, axis, by):
    size = lax.axis_size(axis)
    return lax.ppermute(array, axis, [(i, (i + by) % size) for i in range(size)])


def head_delta(grad_rows, out_rows, heads):
    count = grad_rows.shape[0]
    return jnp.einsum(
        "thd,thd->th",
        grad_rows.reshape(count, heads, HD),
        out_rows.reshape(count, heads, HD),
        preferred_element_type=jnp.float32,
    )


def by_ring(query_act, key_act, value_act, attn_out, grad_out, log_sum, kv_lists):
    head_count = lax.axis_size("head")
    blk_count = lax.axis_size("blk")
    sent_delta = head_delta(grad_out, attn_out, QH)
    query_rows, key_rows, value_rows, grad_rows, total_rows, delta_rows = (
        lax.all_to_all(
            query_act.astype(jnp.float32), "head", split_axis=1, concat_axis=0, tiled=True
        ).astype(query_act.dtype),
        lax.all_to_all(
            key_act.astype(jnp.float32), "head", split_axis=1, concat_axis=0, tiled=True
        ).astype(key_act.dtype),
        lax.all_to_all(
            value_act.astype(jnp.float32), "head", split_axis=1, concat_axis=0, tiled=True
        ).astype(value_act.dtype),
        lax.all_to_all(
            grad_out.astype(jnp.float32), "head", split_axis=1, concat_axis=0, tiled=True
        ).astype(grad_out.dtype),
        lax.all_to_all(log_sum, "head", split_axis=1, concat_axis=0, tiled=True),
        lax.all_to_all(sent_delta, "head", split_axis=1, concat_axis=0, tiled=True),
    )
    tokens = query_rows.shape[0]
    local_heads = KVH // head_count
    group_size = QH // KVH
    blocks_dev = tokens // BLOCK
    scaling = HD ** (-0.5)
    queries = query_rows.reshape(tokens, local_heads, group_size, HD)
    out_grads = grad_rows.reshape(tokens, local_heads, group_size, HD)
    row_totals = total_rows.reshape(tokens, local_heads, group_size).transpose(1, 2, 0)[
        :, :, :, None
    ]
    row_deltas = delta_rows.reshape(tokens, local_heads, group_size).transpose(1, 2, 0)[
        :, :, :, None
    ]
    position = lax.axis_index("blk")
    query_pos = position * tokens + jnp.arange(tokens, dtype=jnp.int32)

    def block_mask(rotation):
        source = (position - rotation) % blk_count
        key_ids = source * blocks_dev + jnp.arange(blocks_dev, dtype=jnp.int32)
        listed = jnp.any(kv_lists[:, :, None] == key_ids[None, None, :], axis=1)
        key_pos = source * tokens + jnp.arange(tokens, dtype=jnp.int32)
        return (listed, key_pos)

    def attend(kv_pair, key_sums, query_grad, listed, key_pos):
        visible = jnp.repeat(jnp.repeat(listed, BLOCK, axis=0), BLOCK, axis=1) & (
            key_pos[None, :] <= query_pos[:, None]
        )
        key_block = kv_pair[0].reshape(tokens, local_heads, HD)
        value_block = kv_pair[1].reshape(tokens, local_heads, HD)
        scores = (
            jnp.einsum("tkgd,skd->kgts", queries, key_block, preferred_element_type=jnp.float32)
            * scaling
        )
        weights = jnp.where(visible, jnp.exp(scores - row_totals), 0.0)
        grad_probs = jnp.einsum(
            "tkgd,skd->kgts", out_grads, value_block, preferred_element_type=jnp.float32
        )
        grad_scores = (weights * (grad_probs - row_deltas)).astype(jnp.bfloat16)
        probs_low = weights.astype(jnp.bfloat16)
        value_part = jnp.einsum(
            "kgts,tkgd->skd", probs_low, out_grads, preferred_element_type=jnp.float32
        )
        key_part = (
            jnp.einsum("kgts,tkgd->skd", grad_scores, queries, preferred_element_type=jnp.float32)
            * scaling
        )
        query_part = (
            jnp.einsum("kgts,skd->tkgd", grad_scores, key_block, preferred_element_type=jnp.float32)
            * scaling
        )
        added = jnp.stack(
            [
                key_part.reshape(tokens, local_heads * HD),
                value_part.reshape(tokens, local_heads * HD),
            ]
        )
        return (key_sums + added, query_grad + query_part)

    def visit(rotation, kv_pair, key_sums, query_grad):
        listed, key_pos = block_mask(rotation)
        return attend(kv_pair, key_sums, query_grad, listed, key_pos)

    kv_pair = jnp.stack([key_rows, value_rows])
    empty_sums = jnp.zeros((2, tokens, local_heads * HD), jnp.float32)
    empty_grad = jnp.zeros((tokens, local_heads, group_size, HD), jnp.float32)

    def advance(rotation, carried):
        kv_here, key_sums, query_grad = carried
        arrived = passed_along(kv_here, "blk", 1)
        key_sums, query_grad = visit(rotation, kv_here, key_sums, query_grad)
        key_sums = shifted(key_sums, "blk", 1)
        return (arrived, key_sums, query_grad)

    kv_here, key_sums, query_grad = lax.fori_loop(
        0, blk_count - 1, advance, (kv_pair, empty_sums, empty_grad)
    )
    key_sums, query_grad = visit(blk_count - 1, kv_here, key_sums, query_grad)
    key_sums = shifted(key_sums.astype(jnp.bfloat16), "blk", 1 - blk_count).astype(key_sums.dtype)
    query_low = query_grad.reshape(tokens, local_heads * group_size * HD).astype(jnp.bfloat16)
    key_low = key_sums[0].astype(jnp.bfloat16)
    value_low = key_sums[1].astype(jnp.bfloat16)
    grad_query, grad_key, grad_value = (
        lax.all_to_all(query_low, "head", split_axis=0, concat_axis=1, tiled=True),
        lax.all_to_all(key_low, "head", split_axis=0, concat_axis=1, tiled=True),
        lax.all_to_all(value_low, "head", split_axis=0, concat_axis=1, tiled=True),
    )
    return (grad_query, grad_key, grad_value)


def local(query_act, *others):
    head_count = lax.axis_size("head")
    blk_count = lax.axis_size("blk")
    if query_act.shape[0] == BLOCK and head_count == 2 and blk_count == 2 * KVH and blk_count * head_count == TREE_B:
        return by_trees(query_act, *others)
    return by_ring(query_act, *others)


def solution(mesh):
    rows = P(("blk", "head"), None)
    return jax.shard_map(
        local,
        mesh=mesh,
        in_specs=(rows,) * 6 + (P("blk", None),),
        out_specs=(rows,) * 3,
        check_vma=False,
    )
```

```python
import functools
import math

import jax
import jax.numpy as jnp
from jax import lax
from jax.experimental import pallas as pl
from jax.experimental.pallas import tpu as pltpu
from jax.sharding import PartitionSpec as P

QH = 40
KVH = 8
HD = 128
BLOCK = 128
TREE_B = 32
GROUP = QH // KVH
SCALING = HD ** (-0.5)
F32 = jnp.float32
BF16 = jnp.bfloat16

Q_ROWS = GROUP * BLOCK
LIST_AT = 2 * BLOCK
KV_ROWS = LIST_AT + 16
X_AT = 2 * Q_ROWS
QG_ROWS = X_AT + 48
COUNT_COL = TREE_B
OWN_COL = TREE_B + 1
VMEM_LIMIT = 14 << 20


def dot_nt(a, b):
    return lax.dot_general(a, b, (((1,), (1,)), ((), ())), preferred_element_type=F32)


def dot_nn(a, b):
    return lax.dot_general(a, b, (((1,), (0,)), ((), ())), preferred_element_type=F32)


def three_parts(array):
    high = array.astype(BF16)
    rest = array - high.astype(F32)
    middle = rest.astype(BF16)
    return high, middle, (rest - middle.astype(F32)).astype(BF16)


def in_vmem(count):
    return [pl.BlockSpec(memory_space=pltpu.VMEM)] * count


def call(kernel, name, in_specs, outs, scratch, micros, args, after=(), limit=VMEM_LIMIT):
    given = len(args)

    def body(*refs):
        kernel(*refs[:given], *refs[given + len(after) :])

    return pl.pallas_call(
        body,
        name=name,
        in_specs=[*in_specs, *[pl.BlockSpec(memory_space=pl.ANY)] * len(after)],
        out_specs=in_vmem(len(outs)),
        out_shape=[jax.ShapeDtypeStruct(*out) for out in outs],
        scratch_shapes=scratch,
        cost_estimate=pl.CostEstimate(flops=int(micros * 1e9), bytes_accessed=int(micros * 3e6), transcendentals=0),
        compiler_params=pltpu.CompilerParams(vmem_limit_bytes=limit),
    )(*args, *after)


def list_row(lists, rows):
    position, parity = lax.axis_index("blk"), lax.axis_index("head")
    me = lax.rem(position, KVH)
    first = (position - me) * 2
    rows[...] = jnp.full(rows.shape, -1.0, F32)
    rows[:2, :TREE_B] = lists[...].astype(F32)
    row = jnp.where(parity == 0, rows[0:1, :], rows[1:2, :])
    seen = row >= 0
    count = jnp.sum(jnp.where(seen, 1.0, 0.0)) - 1.0
    lane = lax.broadcasted_iota(jnp.int32, row.shape, 1)
    row = jnp.where(seen, row - first.astype(F32), -1.0)
    row = jnp.where(lane == COUNT_COL, count, row)
    row = jnp.where(lane == OWN_COL, (2 * me + parity).astype(F32), row)
    return me, jnp.broadcast_to(row, (KV_ROWS - LIST_AT, HD)).astype(BF16)


def kv_pack_kernel(key_in, value_in, lists_in, given, rows, key, value, lists, arrived):
    copies = [
        pltpu.make_async_copy(source, target, arrived.at[i])
        for i, (source, target) in enumerate(((lists_in, lists), (key_in, key), (value_in, value)))
    ]
    for copy in copies:
        copy.start()
    for copy in copies:
        copy.wait()
    me, tile = list_row(lists, rows)
    for i, chip in enumerate(CHIPS):
        columns = pl.ds(pl.multiple_of((me ^ (chip + 1)) * HD, HD), HD)
        given[i, :BLOCK, :] = key[:, columns]
        given[i, BLOCK:LIST_AT, :] = value[:, columns]
        given[i, LIST_AT:, :] = tile


def kv_pack(key_act, value_act, kv_lists):
    outs = [((len(CHIPS), KV_ROWS, HD), BF16)]
    args = (key_act, value_act, kv_lists)
    scratch = [pltpu.VMEM((8, HD), F32), *(pltpu.VMEM(arg.shape, arg.dtype) for arg in args), pltpu.SemaphoreType.DMA((3,))]
    specs = [pl.BlockSpec(memory_space=pl.ANY)] * 3
    return call(kv_pack_kernel, "kv_pack", specs, outs, scratch, 1, args, limit=60 << 20)[0]


def kv_pair_kernel(key, value, lists, theirs, *rest):
    pairs, rows = rest[:-1], rest[-1]
    me, tile = list_row(lists, rows)
    for i, (chip, pair) in enumerate(zip(CHIPS, pairs)):
        columns = pl.ds(pl.multiple_of((me ^ chip) * HD, HD), HD)
        pair[0, :BLOCK, :] = key[:, columns]
        pair[0, BLOCK:LIST_AT, :] = value[:, columns]
        pair[0, LIST_AT:, :] = tile
        pair[1] = theirs[i]


def kv_pair(key_act, value_act, kv_lists, theirs):
    outs = [((2, KV_ROWS, HD), BF16)] * len(CHIPS)
    args = (key_act, value_act, kv_lists, theirs)
    return call(kv_pair_kernel, "kv_pair", in_vmem(4), outs, [pltpu.VMEM((8, HD), F32)], 0.5, args)


def pair_up_kernel(mine, theirs, *pairs):
    for i, pair in enumerate(pairs):
        pair[0] = mine[i]
        pair[1] = theirs[i]


def pair_up(mine, theirs, after=()):
    outs = [((2, *mine.shape[1:]), mine.dtype)] * mine.shape[0]
    return call(pair_up_kernel, "pair_up", in_vmem(2), outs, [], 0.5, (mine, theirs), after)


def pass_on_kernel(source, target):
    target[...] = source[...]


def pass_on(array, after):
    return call(pass_on_kernel, "pass_on", in_vmem(1), [(array.shape, array.dtype)], [], 0.2, (array,), after)[0]


def kv_sum_kernel(mine, theirs, total):
    for i in range(mine.shape[0]):
        total[i] = (mine[i] + theirs[i].astype(F32)).astype(BF16)


def kv_sum(mine, theirs):
    return call(kv_sum_kernel, "kv_sum", in_vmem(2), [(mine.shape, BF16)], [], 0.5, (mine, theirs))[0]


def qg_pack_kernel(slots, query, grad, out, totals, *rest):
    packed, totals_by_group = rest[:-1], rest[-1]
    me = lax.rem(lax.axis_index("blk"), KVH)
    totals_by_group[...] = jnp.zeros(totals_by_group.shape, F32)
    for g in range(KVH):
        totals_by_group[g, :GROUP, :] = totals[g * GROUP : (g + 1) * GROUP, :]
    head_of = lax.broadcasted_iota(jnp.int32, (8, Q_ROWS), 1) // HD
    picks = jnp.where(head_of == lax.broadcasted_iota(jnp.int32, (8, Q_ROWS), 0), 1.0, 0.0).astype(BF16)
    for message, ks in zip(packed, slots):
        for n, k in enumerate(ks):
            columns = pl.ds(pl.multiple_of((me ^ k) * Q_ROWS, Q_ROWS), Q_ROWS)
            queries, grads = query[:, columns], grad[:, columns]
            for h in range(GROUP):
                message[n, h * BLOCK : (h + 1) * BLOCK, :] = queries[:, h * HD : (h + 1) * HD]
                message[n, Q_ROWS + h * BLOCK : Q_ROWS + (h + 1) * BLOCK, :] = grads[:, h * HD : (h + 1) * HD]
            product = grads.astype(F32) * out[:, columns].astype(F32)
            high = product.astype(BF16)
            low = (product - high.astype(F32)).astype(BF16)
            delta = dot_nt(picks, high) + dot_nt(picks, low)
            extras = jnp.concatenate([totals_by_group[me ^ k], delta], axis=0)
            for i, part in enumerate(three_parts(extras)):
                message[n, X_AT + 16 * i : X_AT + 16 * (i + 1), :] = part


def qg_pack(slots, query_act, grad_out, attn_out, totals, after):
    outs = [((len(ks), QG_ROWS, HD), BF16) for ks in slots]
    scratch = [pltpu.VMEM((KVH, 8, HD), F32)]
    args = (query_act, grad_out, attn_out, totals)
    return call(functools.partial(qg_pack_kernel, slots), "qg_pack", in_vmem(4), outs, scratch, 1, args, after)


def attend_kernel(ks, kind, width, *refs):
    refs = list(refs)
    opens, joins, closes = kind == "first", kind in ("join", "last"), kind == "last"
    lists = refs.pop(0)
    messages = []
    while len(messages) < len(ks):
        ref = refs.pop(0)
        messages += [ref.at[n] for n in range(ref.shape[0])]
    if opens:
        kv_own, kv_other = [refs.pop(0) for _ in CHIPS], [refs.pop(0) for _ in CHIPS]
    else:
        keys, keys_t, values, sums_in = (refs.pop(0) for _ in range(4))
    if joins:
        earlier = refs.pop(0)
        backs = [refs.pop(0) for _ in ks]
        for n, back in enumerate(backs):
            back[0] = earlier[n]
        query_grads = [back.at[1] for back in backs]
    else:
        back = refs.pop(0)
        query_grads = [back.at[n] for n in range(len(ks))]
    if closes:
        mine, others = [refs.pop(0) for _ in BACK_HALVES], [refs.pop(0) for _ in BACK_HALVES]
    if opens:
        keys, keys_t, values = (refs.pop(0) for _ in range(3))
    sums = refs.pop(0)
    query_sum, probs_held, scores_held = refs
    me, parity = lists[0, OWN_COL] // 2, lists[0, OWN_COL] % 2
    spare = 2 * KVH

    if opens:
        for own, other, chip in zip(kv_own, kv_other, CHIPS):
            for n in range(2):
                at = 2 * (me ^ (chip + n))
                for ref, j in ((own, at + parity), (other, at + 1 - parity)):
                    keys[j] = ref[n, :BLOCK, :]
                    values[j] = ref[n, BLOCK:LIST_AT, :]
                    keys_t[j] = ref[n, :BLOCK, :].T
        zero = jnp.zeros((BLOCK, HD), BF16)
        keys[spare], keys_t[spare], values[spare] = zero, zero, zero
        sums[...] = jnp.zeros(sums.shape, F32)
    else:
        sums[...] = sums_in[...]

    def both(ref, pair, axis):
        return jnp.concatenate([ref[j] for j in pair], axis=axis)

    def produce(n, pair, extras, diagonal):
        totals, deltas = extras
        scores = dot_nt(both(keys, pair, 0), messages[n][:Q_ROWS, :])
        probs = jnp.exp2(scores * (SCALING * math.log2(math.e)) - totals)
        if diagonal:
            at_key = lax.broadcasted_iota(jnp.int32, probs.shape, 0) - (width - 1) * BLOCK
            at_query = lax.broadcasted_iota(jnp.int32, probs.shape, 1) % BLOCK
            probs = jnp.where(at_key <= at_query, probs, 0.0)
        grad_probs = dot_nt(both(values, pair, 0), messages[n][Q_ROWS:X_AT, :])
        probs_held[...] = probs.astype(BF16)
        scores_held[...] = (probs * (grad_probs - deltas)).astype(BF16)

    def consume(n, pair):
        probs_low, grad_scores = probs_held[...], scores_held[...]
        value_part = dot_nn(probs_low, messages[n][Q_ROWS:X_AT, :])
        key_part = dot_nn(grad_scores, messages[n][:Q_ROWS, :])
        query_sum[...] += dot_nn(both(keys_t, pair, 1), grad_scores)
        for i, j in enumerate(pair):
            sums[j, :BLOCK, :] += key_part[i * BLOCK : (i + 1) * BLOCK, :]
            sums[j, BLOCK:, :] += value_part[i * BLOCK : (i + 1) * BLOCK, :]

    def finish(n):
        for h in range(GROUP):
            part = query_sum[:, h * BLOCK : (h + 1) * BLOCK].T
            query_grads[n][h * BLOCK : (h + 1) * BLOCK, :] = (part * SCALING).astype(BF16)

    pair = None
    for n, k in enumerate(ks):
        parts = [messages[n][X_AT + 16 * i : X_AT + 16 * (i + 1), :].astype(F32) for i in range(3)]
        rows = parts[0] + parts[1] + parts[2]
        totals = jnp.concatenate([rows[h : h + 1, :] for h in range(GROUP)], axis=1) * math.log2(math.e)
        deltas = jnp.concatenate([rows[8 + h : 9 + h, :] for h in range(GROUP)], axis=1)
        extras = (totals, deltas)
        count = lists[k, COUNT_COL]
        steps = count // width
        left = count - steps * width
        first = tuple(
            jnp.where(i < left, lists[k, jnp.minimum(steps * width + i, TREE_B - 1)], spare) for i in range(width - 1)
        ) + (lists[k, OWN_COL],)
        if pair is not None:
            consume(n - 1, pair)
        produce(n, first, extras, True)
        if pair is not None:
            finish(n - 1)
        query_sum[...] = jnp.zeros(query_sum.shape, F32)

        def visit(t, held):
            consume(n, held)
            following = tuple(lists[k, width * t + i] for i in range(width))
            produce(n, following, extras, False)
            return following

        pair = lax.fori_loop(0, steps, visit, first)
    consume(len(ks) - 1, pair)
    finish(len(ks) - 1)

    if closes:
        for half, own, other in zip(BACK_HALVES, mine, others):
            for i, k in enumerate(half):
                at = 2 * (me ^ k)
                own[i, :BLOCK, :] = sums[at + parity, :BLOCK, :] * SCALING
                own[i, BLOCK:, :] = sums[at + parity, BLOCK:, :]
                other[i, :BLOCK, :] = (sums[at + 1 - parity, :BLOCK, :] * SCALING).astype(BF16)
                other[i, BLOCK:, :] = sums[at + 1 - parity, BLOCK:, :].astype(BF16)


def attend(name, kind, ks, width, lists, messages, state, micros):
    blocks = 2 * KVH + 1
    sums = ((blocks, 2 * BLOCK, HD), F32)
    scratch = []
    if kind in ("join", "last"):
        outs = [((2, Q_ROWS, HD), BF16)] * len(ks)
    else:
        outs = [((len(ks), Q_ROWS, HD), BF16)]
    if kind == "first":
        outs += [((blocks, BLOCK, HD), BF16)] * 3
    if kind == "last":
        outs += [((KVH // 2, 2 * BLOCK, HD), kind) for kind in (F32, F32, BF16, BF16)]
        scratch = [pltpu.VMEM(*sums)]
    else:
        outs += [sums]
    scratch += [pltpu.VMEM((HD, Q_ROWS), F32), pltpu.VMEM((width * BLOCK, Q_ROWS), BF16), pltpu.VMEM((width * BLOCK, Q_ROWS), BF16)]
    specs = [pl.BlockSpec(memory_space=pltpu.SMEM)] + in_vmem(len(messages) + len(state))
    kernel = functools.partial(attend_kernel, ks, kind, width)
    return call(kernel, name, specs, outs, scratch, micros, (lists, *messages, *state))


def query_relay_kernel(own, *refs):
    given = refs[-1]
    given[0] = own[1]
    for i, back in enumerate(refs[:-1]):
        given[i + 1] = back[1]


def query_unpack_kernel(*refs):
    backs, theirs, query_grad, done = refs[: len(CHIPS)], *refs[len(CHIPS) :]
    done[...] = jnp.zeros(done.shape, F32)
    me = lax.rem(lax.axis_index("blk"), KVH)
    for i, chip in enumerate(CHIPS):
        for k, ref, n in ((chip, backs[i], 0), (chip + 1, theirs, i)):
            for h in range(GROUP):
                columns = pl.ds(pl.multiple_of(((me ^ k) * GROUP + h) * HD, HD), HD)
                query_grad[:, columns] = ref[n, h * BLOCK : (h + 1) * BLOCK, :]


def kv_unpack_kernel(*refs):
    key_grad, value_grad = refs[len(CHIPS) :]
    me = lax.rem(lax.axis_index("blk"), KVH)
    for i, chip in enumerate(CHIPS):
        for n in range(2):
            columns = pl.ds(pl.multiple_of((me ^ (chip + n)) * HD, HD), HD)
            key_grad[:, columns] = refs[i][n, :BLOCK, :]
            value_grad[:, columns] = refs[i][n, BLOCK:, :]


CHIPS = (0, 2, 4, 6)
CHIPS = (0, 2, 4, 6)
VISITS = (("first", (0, 1)), ("more", (6, 7)), ("more", (2, 4)), ("last", (3, 5)))
EXPECTED = (0.5, 0.5, 0.5, 6)
WIDTHS = (2, 2, 2, 4)
BACK_HALVES = ((1, 3, 5, 7), CHIPS)


def by_trees(query_act, key_act, value_act, attn_out, grad_out, log_sum, kv_lists):
    size = lax.axis_size("blk")

    def exchanged(array, k):
        return lax.ppermute(array, "blk", [(i, i ^ k) for i in range(size)])

    def swapped(array):
        return lax.ppermute(array, "head", [(0, 1), (1, 0)])

    given = kv_pack(key_act, value_act, kv_lists)
    paired = kv_pair(key_act, value_act, kv_lists, exchanged(given, 1))
    kv_own = [paired[0], *(exchanged(part, chip) for part, chip in zip(paired[1:], CHIPS[1:]))]
    kv_other = [swapped(part) for part in kv_own]
    lists = jnp.concatenate([part[:, LIST_AT, : OWN_COL + 1] for part in kv_own]).astype(jnp.int32)

    qg = (query_act, grad_out, attn_out, log_sum.T)
    beside = exchanged(qg_pack(((1, 7),), *qg, (paired[1],))[0], 1)
    own, far = qg_pack(((0,), (6,)), *qg, (kv_other[0],))
    far = pair_up(far, beside[1:], (*kv_own[1:], kv_other[0]))[0]
    here = [[own, beside[:1]], [exchanged(far, 6)]]
    for ks, after in (((2, 4), kv_other[2]), ((3, 5), kv_other[3])):
        sent = qg_pack([(k,) for k in ks], *qg, (after,))
        here.append([exchanged(message, k) for k, message in zip(ks, sent)])

    state, grads = (*kv_own, *kv_other), []
    for i, (kind, ks) in enumerate(VISITS):
        if kind == "last":
            state = (*state, grads[-1])
        results = attend(f"attend_{i}", kind, ks, WIDTHS[i], lists, here[i], state, EXPECTED[i])
        grads.append(results[0])
        state = tuple(results[1:]) if kind == "first" else (*state[:3], results[-1])
    far_back = exchanged(grads[1], 6)
    backs = [exchanged(results[0], 2), exchanged(results[1], 4), far_back]
    others = (pass_on(results[4], (far_back,)), results[5])
    theirs = [swapped(other) for other in others]
    given, kept = [kv_sum(mine, other) for mine, other in zip(results[2:4], theirs)]
    paired = pair_up(kept, exchanged(given, 1))
    kv_back = [paired[0], *(exchanged(pair, chip) for pair, chip in zip(paired[1:], CHIPS[1:]))]
    outs = [((4, Q_ROWS, HD), BF16)]
    given = call(query_relay_kernel, "query_relay", in_vmem(4), outs, [], 0.5, (grads[0], *backs), paired[:1])[0]
    args = (grads[0], *backs, exchanged(given, 1))
    outs = [((BLOCK, QH * HD), BF16), ((8, HD), F32)]
    grad_query, done = call(query_unpack_kernel, "query_unpack", in_vmem(5), outs, [], 1, args)
    outs = [((BLOCK, KVH * HD), BF16)] * 2
    grad_key, grad_value = call(kv_unpack_kernel, "kv_unpack", in_vmem(4), outs, [], 1, kv_back, (done,))
    return grad_query, grad_key, grad_value


def passed_along(array, axis, by):
    size = lax.axis_size(axis)
    pairs = [(i, i + by) for i in range(size) if 0 <= i + by < size]
    return lax.ppermute(array, axis, pairs)


def shifted(array, axis, by):
    size = lax.axis_size(axis)
    return lax.ppermute(array, axis, [(i, (i + by) % size) for i in range(size)])


def head_delta(grad_rows, out_rows, heads):
    count = grad_rows.shape[0]
    return jnp.einsum(
        "thd,thd->th",
        grad_rows.reshape(count, heads, HD),
        out_rows.reshape(count, heads, HD),
        preferred_element_type=jnp.float32,
    )


def by_ring(query_act, key_act, value_act, attn_out, grad_out, log_sum, kv_lists):
    head_count = lax.axis_size("head")
    blk_count = lax.axis_size("blk")
    sent_delta = head_delta(grad_out, attn_out, QH)
    query_rows, key_rows, value_rows, grad_rows, total_rows, delta_rows = (
        lax.all_to_all(
            query_act.astype(jnp.float32), "head", split_axis=1, concat_axis=0, tiled=True
        ).astype(query_act.dtype),
        lax.all_to_all(
            key_act.astype(jnp.float32), "head", split_axis=1, concat_axis=0, tiled=True
        ).astype(key_act.dtype),
        lax.all_to_all(
            value_act.astype(jnp.float32), "head", split_axis=1, concat_axis=0, tiled=True
        ).astype(value_act.dtype),
        lax.all_to_all(
            grad_out.astype(jnp.float32), "head", split_axis=1, concat_axis=0, tiled=True
        ).astype(grad_out.dtype),
        lax.all_to_all(log_sum, "head", split_axis=1, concat_axis=0, tiled=True),
        lax.all_to_all(sent_delta, "head", split_axis=1, concat_axis=0, tiled=True),
    )
    tokens = query_rows.shape[0]
    local_heads = KVH // head_count
    group_size = QH // KVH
    blocks_dev = tokens // BLOCK
    scaling = HD ** (-0.5)
    queries = query_rows.reshape(tokens, local_heads, group_size, HD)
    out_grads = grad_rows.reshape(tokens, local_heads, group_size, HD)
    row_totals = total_rows.reshape(tokens, local_heads, group_size).transpose(1, 2, 0)[
        :, :, :, None
    ]
    row_deltas = delta_rows.reshape(tokens, local_heads, group_size).transpose(1, 2, 0)[
        :, :, :, None
    ]
    position = lax.axis_index("blk")
    query_pos = position * tokens + jnp.arange(tokens, dtype=jnp.int32)

    def block_mask(rotation):
        source = (position - rotation) % blk_count
        key_ids = source * blocks_dev + jnp.arange(blocks_dev, dtype=jnp.int32)
        listed = jnp.any(kv_lists[:, :, None] == key_ids[None, None, :], axis=1)
        key_pos = source * tokens + jnp.arange(tokens, dtype=jnp.int32)
        return (listed, key_pos)

    def attend(kv_pair, key_sums, query_grad, listed, key_pos):
        visible = jnp.repeat(jnp.repeat(listed, BLOCK, axis=0), BLOCK, axis=1) & (
            key_pos[None, :] <= query_pos[:, None]
        )
        key_block = kv_pair[0].reshape(tokens, local_heads, HD)
        value_block = kv_pair[1].reshape(tokens, local_heads, HD)
        scores = (
            jnp.einsum("tkgd,skd->kgts", queries, key_block, preferred_element_type=jnp.float32)
            * scaling
        )
        weights = jnp.where(visible, jnp.exp(scores - row_totals), 0.0)
        grad_probs = jnp.einsum(
            "tkgd,skd->kgts", out_grads, value_block, preferred_element_type=jnp.float32
        )
        grad_scores = (weights * (grad_probs - row_deltas)).astype(jnp.bfloat16)
        probs_low = weights.astype(jnp.bfloat16)
        value_part = jnp.einsum(
            "kgts,tkgd->skd", probs_low, out_grads, preferred_element_type=jnp.float32
        )
        key_part = (
            jnp.einsum("kgts,tkgd->skd", grad_scores, queries, preferred_element_type=jnp.float32)
            * scaling
        )
        query_part = (
            jnp.einsum("kgts,skd->tkgd", grad_scores, key_block, preferred_element_type=jnp.float32)
            * scaling
        )
        added = jnp.stack(
            [
                key_part.reshape(tokens, local_heads * HD),
                value_part.reshape(tokens, local_heads * HD),
            ]
        )
        return (key_sums + added, query_grad + query_part)

    def visit(rotation, kv_pair, key_sums, query_grad):
        listed, key_pos = block_mask(rotation)
        return attend(kv_pair, key_sums, query_grad, listed, key_pos)

    kv_pair = jnp.stack([key_rows, value_rows])
    empty_sums = jnp.zeros((2, tokens, local_heads * HD), jnp.float32)
    empty_grad = jnp.zeros((tokens, local_heads, group_size, HD), jnp.float32)

    def advance(rotation, carried):
        kv_here, key_sums, query_grad = carried
        arrived = passed_along(kv_here, "blk", 1)
        key_sums, query_grad = visit(rotation, kv_here, key_sums, query_grad)
        key_sums = shifted(key_sums, "blk", 1)
        return (arrived, key_sums, query_grad)

    kv_here, key_sums, query_grad = lax.fori_loop(
        0, blk_count - 1, advance, (kv_pair, empty_sums, empty_grad)
    )
    key_sums, query_grad = visit(blk_count - 1, kv_here, key_sums, query_grad)
    key_sums = shifted(key_sums.astype(jnp.bfloat16), "blk", 1 - blk_count).astype(key_sums.dtype)
    query_low = query_grad.reshape(tokens, local_heads * group_size * HD).astype(jnp.bfloat16)
    key_low = key_sums[0].astype(jnp.bfloat16)
    value_low = key_sums[1].astype(jnp.bfloat16)
    grad_query, grad_key, grad_value = (
        lax.all_to_all(query_low, "head", split_axis=0, concat_axis=1, tiled=True),
        lax.all_to_all(key_low, "head", split_axis=0, concat_axis=1, tiled=True),
        lax.all_to_all(value_low, "head", split_axis=0, concat_axis=1, tiled=True),
    )
    return (grad_query, grad_key, grad_value)


def local(query_act, *others):
    head_count = lax.axis_size("head")
    blk_count = lax.axis_size("blk")
    if query_act.shape[0] == BLOCK and head_count == 2 and blk_count == 2 * KVH and blk_count * head_count == TREE_B:
        return by_trees(query_act, *others)
    return by_ring(query_act, *others)


def solution(mesh):
    rows = P(("blk", "head"), None)
    return jax.shard_map(
        local,
        mesh=mesh,
        in_specs=(rows,) * 6 + (P("blk", None),),
        out_specs=(rows,) * 3,
        check_vma=False,
    )
```
